512 devices in a mesh: inst: 64 (over x_hi, z, core), tp: 8 (over x_lo, y).
Axes of the slice: x: 4 (x_hi: 2, x_lo: 2; x = x_hi * 2 + x_lo), y: 4, z: 16, core: 2. Of those that a mesh axis runs over, the one named last changes fastest.
Arguments:
- queries: bfloat16 [8192, 8192], P('inst', 'tp'), may hold values from -12 to 12
- span_keys: bfloat16 [8192, 1024], P('inst', 'tp'), may hold values from -12 to 12
- span_values: bfloat16 [8192, 1024], P('inst', 'tp'), may hold values from -6 to 6
- prefix_keys: bfloat16 [4096, 1024], P(('inst', 'tp')), may hold values from -6 to 6
- prefix_values: bfloat16 [4096, 1024], P(('inst', 'tp')), may hold values from -6 to 6
- span_seg: int32 [8192], replicated, may hold values from 0 to 3, never falling along the last dimension, each value on 1 to 4096 neighbouring positions
- prefix_lengths: int32 [4], replicated, may hold values from 1 to 2048, 4096 in all
Outputs:
- attended: bfloat16 [8192, 8192], P('inst', 'tp')
The draws below stay inside these ranges and needn't reach their ends.
Inputs may be any that keep to these rules, and one draw needn't show every extreme that they name: `span_seg`: requests in order along the block, never falling; each of the 4 requests has 1 to 4096 tokens and one has exactly 4096. `prefix_lengths`: the prefixes lie end to end in request order and sum to 4096; one has exactly 2048.
All inputs are finite; a program needn't handle non-finite values.
Results may differ from the reference program's by a relative error of at most 0.0085.
Values may be sent and summed in bfloat16 or wider, within the bound.
No kernel may reach another device: no remote copies, remote signals or barrier semaphores. Data moves between devices by JAX's collectives and lax.ppermute only.
A program may use at most 128 MiB of HBM per device.

```python
import math
import jax
import jax.numpy as jnp
import numpy as np
from jax import lax

HEADS = 64
KV_HEADS = 8
HD = 128
REQ = 4
SPAN = 8192
PREFIX = 4096
SEG_MOST = 4096
PRE_MOST = 2048


def draw_queries(key, part):
    key = jax.random.fold_in(key, 5)
    values = jnp.clip(jax.random.normal(key, (SPAN, HEADS * HD), jnp.float32), -6.0, 6.0)
    return values.astype(jnp.bfloat16)


def draw_span_keys(key, part):
    key = jax.random.fold_in(key, 9)
    values = jnp.clip(jax.random.normal(key, (SPAN, KV_HEADS * HD), jnp.float32), -6.0, 6.0)
    return values.astype(jnp.bfloat16)


def block_levels(rng, dims, split, smallest, largest):
    def one(axis_at, blocks):
        draws = jax.random.uniform(jax.random.fold_in(jax.random.fold_in(rng, 6), axis_at), (blocks,), jnp.float32, smallest / len(split), largest / len(split))
        return jnp.repeat(jnp.exp(draws), dims[axis_at] // blocks).reshape((-1,) + (1,) * (len(dims) - axis_at - 1))

    level = one(*split[0])
    for cut in split[1:]:
        level = level * one(*cut)
    return level


def length_profile(amount, total, limit, lean):
    loads = [(1 << 20) // math.isqrt(standing ** lean) + 1 for standing in range(2, amount + 1)]
    surplus, holding = total - limit - (amount - 1), [1] * (amount - 1)
    while surplus > 0:
        candidates = [i for i in range(amount - 1) if holding[i] < limit]
        pool, budget = sum([loads[i] for i in candidates]), surplus
        for i in candidates:
            more = min(limit - holding[i], max(1, budget * loads[i] // pool), surplus)
            holding[i] = holding[i] + more
            surplus = surplus - more
    return np.array([limit] + holding)


def ragged(key, count, total, reach, slope):
    if count == 2:
        one = jax.random.randint(key, (), max(1, total - reach), min(reach, total - 1) + 1)
        return jnp.stack([one, total - one])
    sizes = jnp.asarray(length_profile(count, total, reach, slope), jnp.int32)
    couples = (count - 1) // 2
    donor, sink = sizes[1:1 + 2 * couples:2], sizes[2:2 + 2 * couples:2]
    room = jnp.minimum(donor - 1, reach - sink)
    shifted = jax.random.randint(jax.random.fold_in(key, 1), (couples,), 0, 1 << 20) % (room + 1)
    sizes = sizes.at[1:1 + 2 * couples:2].set(donor - shifted).at[2:2 + 2 * couples:2].set(sink + shifted)
    return sizes[jax.random.permutation(jax.random.fold_in(key, 2), count)]


def gaussian(stream_key, dims, width, bound, shards=(), kind=jnp.bfloat16):
    entries = width * jax.random.normal(stream_key, dims, jnp.float32)
    if shards:
        entries = entries * block_levels(stream_key, dims, shards, -0.22, 0.18)
    return jnp.clip(entries, -bound, bound).astype(kind)


def setup_inputs(seed: int = 0) -> dict:
    arg_keys = jax.random.split(jax.random.key(seed), 8)
    queries = draw_queries(jax.random.fold_in(arg_keys[7], 71), 0)
    span_keys = draw_span_keys(jax.random.fold_in(arg_keys[7], 71), 0)
    span_values = gaussian(arg_keys[2], (SPAN, KV_HEADS * HD), 1.0, 6.0, ((0, 64), (1, 8)))
    prefix_keys = gaussian(arg_keys[3], (PREFIX, KV_HEADS * HD), 1.0, 6.0, ((0, 512),))
    prefix_values = gaussian(arg_keys[4], (PREFIX, KV_HEADS * HD), 1.0, 6.0, ((0, 512),))
    span_seg = jnp.searchsorted(jnp.cumsum(ragged(arg_keys[5], REQ, SPAN, SEG_MOST, 2)), jnp.arange(SPAN), side="right").astype(jnp.int32)
    prefix_lengths = ragged(arg_keys[6], REQ, PREFIX, PRE_MOST, 2).astype(jnp.int32)
    return {"queries": queries, "span_keys": span_keys, "span_values": span_values, "prefix_keys": prefix_keys, "prefix_values": prefix_values, "span_seg": span_seg, "prefix_lengths": prefix_lengths}


def reference(queries, span_keys, span_values, prefix_keys, prefix_values, span_seg, prefix_lengths):
    group = HEADS // KV_HEADS
    scale = 1.0 / math.sqrt(HD)
    ends = jnp.cumsum(prefix_lengths).astype(jnp.int32)
    starts = (ends - prefix_lengths).astype(jnp.int32)
    total_keys = PREFIX + SPAN
    keys_all = jnp.concatenate([prefix_keys, span_keys], 0).astype(jnp.float32).reshape(total_keys, KV_HEADS, HD)
    vals_all = jnp.concatenate([prefix_values, span_values], 0).astype(jnp.float32).reshape(total_keys, KV_HEADS, HD)
    prefix_pos = jnp.arange(PREFIX, dtype=jnp.int32)
    span_pos = jnp.arange(SPAN, dtype=jnp.int32)
    lower = jnp.take(starts, span_seg)
    upper = jnp.take(ends, span_seg)
    block = 512

    def per_block(index):
        first = (index * block).astype(jnp.int32)
        rows = lax.dynamic_slice_in_dim(queries, first, block, 0).astype(jnp.float32)
        rows = rows.reshape(block, KV_HEADS, group, HD)
        seg_rows = lax.dynamic_slice_in_dim(span_seg, first, block, 0)
        low_rows = lax.dynamic_slice_in_dim(lower, first, block, 0)
        high_rows = lax.dynamic_slice_in_dim(upper, first, block, 0)
        pos_rows = first + jnp.arange(block, dtype=jnp.int32)
        mask_prefix = (prefix_pos[None, :] >= low_rows[:, None]) & (prefix_pos[None, :] < high_rows[:, None])
        mask_span = (span_seg[None, :] == seg_rows[:, None]) & (span_pos[None, :] <= pos_rows[:, None])
        mask = jnp.concatenate([mask_prefix, mask_span], 1)

        def per_head(head):
            keys = keys_all[:, head, :]
            vals = vals_all[:, head, :]
            query = rows[:, head]
            scores = jnp.einsum('bgd,kd->bgk', query, keys) * scale
            scores = jnp.where(mask[:, None, :], scores, -jnp.inf)
            top = lax.optimization_barrier(jnp.max(scores, axis=-1))
            expo = jnp.exp(scores - top[..., None])
            total = lax.optimization_barrier(jnp.sum(expo, axis=-1))
            weights = expo.astype(jnp.bfloat16).astype(jnp.float32)
            summed = jnp.einsum('bgk,kd->bgd', weights, vals)
            return summed / total[..., None]
        outs = lax.map(per_head, jnp.arange(KV_HEADS, dtype=jnp.int32))
        outs = jnp.transpose(outs, (1, 0, 2, 3)).reshape(block, HEADS * HD)
        return outs.astype(jnp.bfloat16)
    result = lax.map(per_block, jnp.arange(SPAN // block, dtype=jnp.int32))
    return result.reshape(SPAN, HEADS * HD)
```

```python
import functools
import math

import jax
import jax.numpy as jnp
from jax import lax
from jax.experimental import pallas as pl
from jax.experimental.pallas import tpu as pltpu
from jax.sharding import Mesh, PartitionSpec as P

HEADS = 64
KV_HEADS = 8
HD = 128
GROUP = HEADS // KV_HEADS
REQ = 4
SPAN = 8192
PREFIX = 4096
XH, Z, CORE, TP = 2, 16, 2, 8
CHIPS = XH * Z
INST = ("xh", "z", "core")
ROWS = SPAN // (CHIPS * CORE)
KEYS = ROWS * CORE
PIECE = PREFIX // CHIPS
BLOCK_ROWS = KEYS + XH * PIECE
LANES = 2 * ROWS
PARTS = GROUP * ROWS // LANES
STEPS = Z // 2
STATE_ROWS = HD + 8
LOW = -1e30
EXP2_SCALE = math.log2(math.e) / math.sqrt(HD)

SMEM = pl.BlockSpec(memory_space=pltpu.SMEM)
VMEM = pl.BlockSpec(memory_space=pltpu.VMEM)
PARAMS = pltpu.CompilerParams(vmem_limit_bytes=24 * 1024 * 1024)


def pack(place_ref, own_ref, first_ref, second_ref, pre_ref, block_ref):
    core = place_ref[2]

    @pl.when(core == 0)
    def _():
        for i, ref in enumerate((own_ref, first_ref)):
            for j in range(2):
                block_ref[i * ROWS : (i + 1) * ROWS, j * HD : (j + 1) * HD] = ref[j]

    @pl.when(core != 0)
    def _():
        for i, ref in enumerate((first_ref, second_ref)):
            for j in range(2):
                block_ref[i * ROWS : (i + 1) * ROWS, j * HD : (j + 1) * HD] = ref[j]

    block_ref[KEYS:, :] = pre_ref[...]


def plan(place_ref, lengths_ref, seg_ref, q_ref, sib_ref, scalars_ref, bounds_ref, rows_ref):
    inst = (place_ref[0] * Z + place_ref[1]) * CORE + place_ref[2]
    sibling = inst + 1 - 2 * place_ref[2]
    seg = seg_ref[...]
    counts = [jnp.int32(0)] + [
        jnp.sum(jnp.where(seg < s, 1.0, 0.0)).astype(jnp.int32) for s in range(1, REQ)
    ]
    starts, ends, running = [], [], jnp.int32(0)
    for s in range(REQ):
        starts.append(running)
        running = running + lengths_ref[s]
        ends.append(running)

    def pick(values, s):
        out = values[0]
        for k in range(1, REQ):
            out = jnp.where(s == k, values[k], out)
        return out

    for half, block in enumerate((inst, sibling)):
        first = block * ROWS
        first_seg, last_seg = jnp.int32(0), jnp.int32(0)
        for s in range(1, REQ):
            first_seg = first_seg + (first >= counts[s]).astype(jnp.int32)
            last_seg = last_seg + (first + ROWS - 1 >= counts[s]).astype(jnp.int32)
        values = (
            pick(starts, first_seg), pick(ends, last_seg), pick(starts, last_seg), pick(ends, first_seg),
            pick(counts, first_seg), first + ROWS, pick(counts, last_seg), first + 1,
        )
        for i, value in enumerate(values):
            scalars_ref[half * 8 + i] = value
        position = first + lax.broadcasted_iota(jnp.int32, (1, ROWS), 1)
        row_seg = jnp.zeros((1, ROWS), jnp.int32)
        for s in range(1, REQ):
            row_seg = row_seg + jnp.where(position >= counts[s], 1, 0)
        bounds_ref[half, 0:1, :] = pick(starts, row_seg)
        bounds_ref[half, 1:2, :] = pick(ends, row_seg)
        bounds_ref[half, 2:3, :] = pick(counts, row_seg)
        bounds_ref[half, 3:4, :] = position + 1
        ref = (q_ref, sib_ref)[half]
        for h in range(GROUP):
            rows_ref[half, h // 2, h % 2 * ROWS : (h % 2 + 1) * ROWS, :] = ref[:, h * HD : (h + 1) * HD]


def absorb_step(step, final, place_ref, scalars_ref, bounds_ref, rows_ref, block_ref, *refs):
    if final:
        before, own_ref, sib_ref, state = refs
        state[...] = before[...]
    elif step:
        before, state = refs
        state[...] = before[...]
    else:
        (state,) = refs
        state[:, :, :HD, :] = jnp.zeros((CORE, PARTS, HD, LANES), jnp.float32)
        state[:, :, HD:, :] = jnp.zeros((CORE, PARTS, STATE_ROWS - HD, LANES), jnp.float32)
        state[:, :, HD : HD + 1, :] = jnp.full((CORE, PARTS, 1, LANES), LOW, jnp.float32)
    core = place_ref[2]
    chip = place_ref[0] * Z + place_ref[1]
    origin = lax.rem(jnp.where(core == 0, chip - step + CHIPS, chip + Z + step), CHIPS)

    def absorb(half, row, count, base, kind, masked):
        keys = block_ref[pl.ds(row, count), :HD]
        vals = block_ref[pl.ds(row, count), HD:]
        if masked:
            index = base + lax.broadcasted_iota(jnp.int32, (count, ROWS), 0)
            low = bounds_ref[half, 2 * kind : 2 * kind + 1, :]
            high = bounds_ref[half, 2 * kind + 1 : 2 * kind + 2, :]
            bias = jnp.where((index >= low) & (index < high), 0.0, LOW)
            bias = jnp.concatenate([bias] * (LANES // ROWS), axis=1)
        for b in range(PARTS):
            scores = lax.dot_general(
                keys, rows_ref[half, b], (((1,), (1,)), ((), ())), preferred_element_type=jnp.float32
            )
            if masked:
                scores = scores + bias
            old = state[half, b, HD : HD + 1, :]
            new = jnp.maximum(old, jnp.max(scores, axis=0, keepdims=True))
            factor = jnp.exp2((old - new) * EXP2_SCALE)
            expo = jnp.exp2((scores - new) * EXP2_SCALE)
            total = state[half, b, HD + 1 : HD + 2, :] * factor + jnp.sum(expo, axis=0, keepdims=True)
            state[half, b, HD : HD + 1, :] = new
            state[half, b, HD + 1 : HD + 2, :] = total
            state[half, b, :HD, :] = state[half, b, :HD, :] * factor + lax.dot_general(
                vals, expo.astype(jnp.bfloat16), (((0,), (0,)), ((), ())), preferred_element_type=jnp.float32
            )

    def visit(half, row, count, base, kind, wanted):
        least_lo, most_hi, most_lo, least_hi = [scalars_ref[half * 8 + kind * 4 + i] for i in range(4)]
        seen = wanted & (base < most_hi) & (base + count > least_lo)
        whole = (base >= most_lo) & (base + count <= least_hi)

        @pl.when(seen & whole)
        def _():
            absorb(half, row, count, base, kind, False)

        @pl.when(seen & jnp.logical_not(whole))
        def _():
            absorb(half, row, count, base, kind, True)

    def one_half(half, carry):
        visit(half, 0, KEYS, origin * KEYS, 1, (core == 0) | (step < STEPS))

        def one_piece(xh, carry):
            row = pl.multiple_of(KEYS + xh * PIECE, PIECE)
            base = (xh * Z + lax.rem(origin, Z)) * PIECE
            visit(half, row, PIECE, base, 0, (core == 0) | (0 < step < STEPS))
            return carry

        return lax.fori_loop(0, XH, one_piece, carry)

    lax.fori_loop(0, CORE, one_half, 0)
    if final:
        own_ref[...] = state[0]
        sib_ref[...] = state[1]


def merge(own_ref, other_ref, out_ref):
    for b in range(PARTS):
        top_a, top_b = own_ref[b, HD : HD + 1, :], other_ref[b, HD : HD + 1, :]
        top = jnp.maximum(top_a, top_b)
        factor_a = jnp.exp2((top_a - top) * EXP2_SCALE)
        factor_b = jnp.exp2((top_b - top) * EXP2_SCALE)
        total = own_ref[b, HD + 1 : HD + 2, :] * factor_a + other_ref[b, HD + 1 : HD + 2, :] * factor_b
        result = (own_ref[b, :HD, :] * factor_a + other_ref[b, :HD, :] * factor_b) / total
        for i in range(LANES // ROWS):
            h = b * (LANES // ROWS) + i
            out_ref[:, h * HD : (h + 1) * HD] = result[:, i * ROWS : (i + 1) * ROWS].T.astype(jnp.bfloat16)


STATE = jax.ShapeDtypeStruct((CORE, PARTS, STATE_ROWS, LANES), jnp.float32)
HALF_STATE = jax.ShapeDtypeStruct((PARTS, STATE_ROWS, LANES), jnp.float32)


def call_pack(place, own, first, second, pre):
    return pl.pallas_call(
        pack,
        out_shape=jax.ShapeDtypeStruct((BLOCK_ROWS, 2 * HD), jnp.bfloat16),
        in_specs=[SMEM, VMEM, VMEM, VMEM, VMEM],
        out_specs=VMEM,
        compiler_params=PARAMS,
        name="pack",
    )(place, own, first, second, pre)


def call_plan(place, prefix_lengths, span_seg, queries, sib_queries):
    return pl.pallas_call(
        plan,
        out_shape=(
            jax.ShapeDtypeStruct((CORE * 8,), jnp.int32),
            jax.ShapeDtypeStruct((CORE, 8, ROWS), jnp.int32),
            jax.ShapeDtypeStruct((CORE, PARTS, LANES, HD), jnp.bfloat16),
        ),
        in_specs=[SMEM, SMEM, VMEM, VMEM, VMEM],
        out_specs=(SMEM, VMEM, VMEM),
        compiler_params=PARAMS,
        name="plan",
    )(place, prefix_lengths, span_seg.reshape(-1, ROWS), queries, sib_queries)


def call_absorb(step, place, planned, block, state):
    final = step == STEPS
    return pl.pallas_call(
        functools.partial(absorb_step, step, final),
        out_shape=(HALF_STATE, HALF_STATE) if final else STATE,
        in_specs=[SMEM, SMEM, VMEM, VMEM, VMEM] + ([VMEM] if step else []),
        out_specs=(VMEM, VMEM) if final else VMEM,
        scratch_shapes=[pltpu.VMEM(STATE.shape, STATE.dtype)] if final else [],
        compiler_params=PARAMS,
        cost_estimate=pl.CostEstimate(flops=537_000_000, bytes_accessed=3_000_000, transcendentals=1_050_000),
        name="absorb",
    )(place, *planned, block, *([state] if step else []))


def call_merge(own, other):
    return pl.pallas_call(
        merge,
        out_shape=jax.ShapeDtypeStruct((ROWS, GROUP * HD), jnp.bfloat16),
        in_specs=[VMEM, VMEM],
        out_specs=VMEM,
        compiler_params=PARAMS,
        name="merge",
    )(own, other)


def at(xh, z, core):
    return (xh * Z + z) * CORE + core


def body(queries, span_keys, span_values, prefix_keys, prefix_values, span_seg, prefix_lengths):
    place = jnp.stack([lax.axis_index(a) for a in INST]).astype(jnp.int32)
    everyone = [(xh, z) for xh in range(XH) for z in range(Z)]
    cores = [(at(xh, z, c), at(xh, z, 1 - c)) for xh, z in everyone for c in range(CORE)]
    one = [(at(xh, z, 1), at(xh, z, 0)) for xh, z in everyone] + [(at(xh, z, 0), at(1 - xh, z, 1)) for xh, z in everyone]
    two = [(at(xh, z, 1), at(1 - xh, z, 1)) for xh, z in everyone]
    onward = [(c * CORE, (c + 1) % CHIPS * CORE) for c in range(CHIPS)]
    back = [(c * CORE + 1, (c - 1) % CHIPS * CORE + 1) for c in range(CHIPS)]

    span = jnp.stack([span_keys, span_values])
    first = lax.ppermute(span, INST, one)
    second = lax.ppermute(span, INST, two)
    sib_queries = lax.ppermute(queries, INST, cores)

    pre = jnp.concatenate(
        [prefix_keys.reshape(-1, KV_HEADS, HD), prefix_values.reshape(-1, KV_HEADS, HD)], axis=2
    ).transpose(1, 0, 2)
    pre = jnp.broadcast_to(pre[None], (XH * CORE,) + pre.shape).reshape((XH * CORE * TP,) + pre.shape[1:])
    pre = lax.all_to_all(pre, ("xh", "core", "tp"), split_axis=0, concat_axis=0, tiled=True)
    pre = pre.reshape(XH * PIECE, 2 * HD)

    block = call_pack(place, span, first, second, pre)
    planned = call_plan(place, prefix_lengths, span_seg, queries, sib_queries)
    state = None
    for step in range(STEPS + 1):
        if step < STEPS:
            arriving = lax.ppermute(block, INST, onward + back if step < STEPS - 1 else onward)
        state = call_absorb(step, place, planned, block, state)
        if step < STEPS:
            block, state = lax.optimization_barrier((arriving, state))
    own, sib = state
    return call_merge(own, lax.ppermute(sib, INST, cores))


def solution(mesh):
    cut = Mesh(mesh.devices.reshape(XH, Z, CORE, TP), INST + ("tp",))
    in_specs = (
        P(INST, "tp"),
        P(INST, "tp"),
        P(INST, "tp"),
        P(INST + ("tp",), None),
        P(INST + ("tp",), None),
        P(),
        P(),
    )
    return jax.shard_map(body, mesh=cut, in_specs=in_specs, out_specs=P(INST, "tp"), check_vma=False)
```

```python
import functools
import math

import jax
import jax.numpy as jnp
from jax import lax
from jax.experimental import pallas as pl
from jax.experimental.pallas import tpu as pltpu
from jax.sharding import Mesh, PartitionSpec as P

HEADS = 64
KV_HEADS = 8
HD = 128
GROUP = HEADS // KV_HEADS
REQ = 4
SPAN = 8192
PREFIX = 4096
XH, Z, CORE, TP = 2, 16, 2, 8
CHIPS = XH * Z
INST = ("xh", "z", "core")
ROWS = SPAN // (CHIPS * CORE)
KEYS = ROWS * CORE
PIECE = PREFIX // CHIPS
HALF_ROWS = KEYS + PIECE
BLOCK_ROWS = XH * HALF_ROWS
LANES = 2 * ROWS
PARTS = GROUP * ROWS // LANES
STEPS = Z // 2
STATE_ROWS = HD + 8
LOW = -1e30
EXP2_SCALE = math.log2(math.e) / math.sqrt(HD)

SMEM = pl.BlockSpec(memory_space=pltpu.SMEM)
VMEM = pl.BlockSpec(memory_space=pltpu.VMEM)
PARAMS = pltpu.CompilerParams(vmem_limit_bytes=24 * 1024 * 1024)


def lay(keys_ref, vals_ref, pre_keys_ref, pre_vals_ref, span_ref, pre_ref):
    for i in range(XH * CORE):
        span_ref[i, :, :HD] = keys_ref[...]
        span_ref[i, :, HD:] = vals_ref[...]
        for t in range(TP):
            pre_ref[i, t, :, :HD] = pre_keys_ref[:, t * HD : (t + 1) * HD]
            pre_ref[i, t, :, HD:] = pre_vals_ref[:, t * HD : (t + 1) * HD]


def pack(span_ref, pre_ref, block_ref):
    for xh in range(XH):
        block_ref[xh * HALF_ROWS : xh * HALF_ROWS + KEYS, :] = span_ref[xh * KEYS : (xh + 1) * KEYS, :]
        block_ref[xh * HALF_ROWS + KEYS : (xh + 1) * HALF_ROWS, :] = pre_ref[xh * PIECE : (xh + 1) * PIECE, :]


def plan(place_ref, lengths_ref, seg_ref, q_ref, sib_ref, scalars_ref, bounds_ref, rows_ref):
    inst = (place_ref[0] * Z + place_ref[1]) * CORE + place_ref[2]
    sibling = inst + 1 - 2 * place_ref[2]
    seg = seg_ref[...]
    counts = [jnp.int32(0)] + [
        jnp.sum(jnp.where(seg < s, 1.0, 0.0)).astype(jnp.int32) for s in range(1, REQ)
    ]
    starts, ends, running = [], [], jnp.int32(0)
    for s in range(REQ):
        starts.append(running)
        running = running + lengths_ref[s]
        ends.append(running)

    def pick(values, s):
        out = values[0]
        for k in range(1, REQ):
            out = jnp.where(s == k, values[k], out)
        return out

    for half, block in enumerate((inst, sibling)):
        first = block * ROWS
        first_seg, last_seg = jnp.int32(0), jnp.int32(0)
        for s in range(1, REQ):
            first_seg = first_seg + (first >= counts[s]).astype(jnp.int32)
            last_seg = last_seg + (first + ROWS - 1 >= counts[s]).astype(jnp.int32)
        values = (
            pick(starts, first_seg), pick(ends, last_seg), pick(starts, last_seg), pick(ends, first_seg),
            pick(counts, first_seg), first + ROWS, pick(counts, last_seg), first + 1,
        )
        for i, value in enumerate(values):
            scalars_ref[half * 8 + i] = value
        position = first + lax.broadcasted_iota(jnp.int32, (1, ROWS), 1)
        row_seg = jnp.zeros((1, ROWS), jnp.int32)
        for s in range(1, REQ):
            row_seg = row_seg + jnp.where(position >= counts[s], 1, 0)
        bounds_ref[half, 0:1, :] = pick(starts, row_seg)
        bounds_ref[half, 1:2, :] = pick(ends, row_seg)
        bounds_ref[half, 2:3, :] = pick(counts, row_seg)
        bounds_ref[half, 3:4, :] = position + 1
        ref = (q_ref, sib_ref)[half]
        for h in range(GROUP):
            rows_ref[half, h // 2, h % 2 * ROWS : (h % 2 + 1) * ROWS, :] = ref[:, h * HD : (h + 1) * HD]


def absorb_step(step, final, place_ref, scalars_ref, bounds_ref, rows_ref, block_ref, *refs):
    if final:
        before, own_ref, sib_ref, state = refs
        state[...] = before[...]
    elif step:
        before, state = refs
        state[...] = before[...]
    else:
        (state,) = refs
        state[:, :, :HD, :] = jnp.zeros((CORE, PARTS, HD, LANES), jnp.float32)
        state[:, :, HD:, :] = jnp.zeros((CORE, PARTS, STATE_ROWS - HD, LANES), jnp.float32)
        state[:, :, HD : HD + 1, :] = jnp.full((CORE, PARTS, 1, LANES), LOW, jnp.float32)
    core, z = place_ref[2], place_ref[1]
    origin = lax.rem(jnp.where(core == 0, z - step + Z, z + step), Z)

    def absorb(half, row, count, base, kind, masked):
        keys = block_ref[pl.ds(row, count), :HD]
        vals = block_ref[pl.ds(row, count), HD:]
        if masked:
            index = base + lax.broadcasted_iota(jnp.int32, (count, ROWS), 0)
            low = bounds_ref[half, 2 * kind : 2 * kind + 1, :]
            high = bounds_ref[half, 2 * kind + 1 : 2 * kind + 2, :]
            bias = jnp.where((index >= low) & (index < high), 0.0, LOW)
            bias = jnp.concatenate([bias] * (LANES // ROWS), axis=1)
        for b in range(PARTS):
            scores = lax.dot_general(
                keys, rows_ref[half, b], (((1,), (1,)), ((), ())), preferred_element_type=jnp.float32
            )
            if masked:
                scores = scores + bias
            old = state[half, b, HD : HD + 1, :]
            new = jnp.maximum(old, jnp.max(scores, axis=0, keepdims=True))
            factor = jnp.exp2((old - new) * EXP2_SCALE)
            expo = jnp.exp2((scores - new) * EXP2_SCALE)
            total = state[half, b, HD + 1 : HD + 2, :] * factor + jnp.sum(expo, axis=0, keepdims=True)
            state[half, b, HD : HD + 1, :] = new
            state[half, b, HD + 1 : HD + 2, :] = total
            state[half, b, :HD, :] = state[half, b, :HD, :] * factor + lax.dot_general(
                vals, expo.astype(jnp.bfloat16), (((0,), (0,)), ((), ())), preferred_element_type=jnp.float32
            )

    def visit(half, row, count, base, kind):
        least_lo, most_hi, most_lo, least_hi = [scalars_ref[half * 8 + kind * 4 + i] for i in range(4)]
        seen = (base < most_hi) & (base + count > least_lo)
        whole = (base >= most_lo) & (base + count <= least_hi)

        @pl.when(seen & whole)
        def _():
            absorb(half, row, count, base, kind, False)

        @pl.when(seen & jnp.logical_not(whole))
        def _():
            absorb(half, row, count, base, kind, True)

    def visit_both(half, xh, row):
        visit(half, pl.multiple_of(row, PIECE), KEYS, (xh * Z + origin) * KEYS, 1)
        visit(half, pl.multiple_of(row + KEYS, PIECE), PIECE, (xh * Z + origin) * PIECE, 0)

    def one_half(half, carry):
        if step == 0:
            visit_both(half, core, core * HALF_ROWS)
        elif final:
            visit_both(half, core, 0)
        else:

            def one_xh(xh, carry):
                visit_both(half, xh, xh * HALF_ROWS)
                return carry

            lax.fori_loop(0, XH, one_xh, 0)
        return carry

    lax.fori_loop(0, CORE, one_half, 0)
    if final:
        own_ref[...] = state[0]
        sib_ref[...] = state[1]


def merge(own_ref, other_ref, out_ref):
    for b in range(PARTS):
        top_a, top_b = own_ref[b, HD : HD + 1, :], other_ref[b, HD : HD + 1, :]
        top = jnp.maximum(top_a, top_b)
        factor_a = jnp.exp2((top_a - top) * EXP2_SCALE)
        factor_b = jnp.exp2((top_b - top) * EXP2_SCALE)
        total = own_ref[b, HD + 1 : HD + 2, :] * factor_a + other_ref[b, HD + 1 : HD + 2, :] * factor_b
        result = (own_ref[b, :HD, :] * factor_a + other_ref[b, :HD, :] * factor_b) / total
        for i in range(LANES // ROWS):
            h = b * (LANES // ROWS) + i
            out_ref[:, h * HD : (h + 1) * HD] = result[:, i * ROWS : (i + 1) * ROWS].T.astype(jnp.bfloat16)


STATE = jax.ShapeDtypeStruct((CORE, PARTS, STATE_ROWS, LANES), jnp.float32)
HALF_STATE = jax.ShapeDtypeStruct((PARTS, STATE_ROWS, LANES), jnp.float32)


def call_lay(span_keys, span_values, prefix_keys, prefix_values):
    return pl.pallas_call(
        lay,
        out_shape=(
            jax.ShapeDtypeStruct((XH * CORE, ROWS, 2 * HD), jnp.bfloat16),
            jax.ShapeDtypeStruct((XH * CORE, TP, prefix_keys.shape[0], 2 * HD), jnp.bfloat16),
        ),
        in_specs=[VMEM] * 4,
        out_specs=(VMEM, VMEM),
        compiler_params=PARAMS,
        name="lay",
    )(span_keys, span_values, prefix_keys, prefix_values)


def call_pack(span, pre):
    return pl.pallas_call(
        pack,
        out_shape=jax.ShapeDtypeStruct((BLOCK_ROWS, 2 * HD), jnp.bfloat16),
        in_specs=[VMEM, VMEM],
        out_specs=VMEM,
        compiler_params=PARAMS,
        name="pack",
    )(span, pre)


def call_plan(place, prefix_lengths, span_seg, queries, sib_queries):
    return pl.pallas_call(
        plan,
        out_shape=(
            jax.ShapeDtypeStruct((CORE * 8,), jnp.int32),
            jax.ShapeDtypeStruct((CORE, 8, ROWS), jnp.int32),
            jax.ShapeDtypeStruct((CORE, PARTS, LANES, HD), jnp.bfloat16),
        ),
        in_specs=[SMEM, SMEM, VMEM, VMEM, VMEM],
        out_specs=(SMEM, VMEM, VMEM),
        compiler_params=PARAMS,
        name="plan",
    )(place, prefix_lengths, span_seg.reshape(-1, ROWS), queries, sib_queries)


def call_absorb(step, place, planned, block, state):
    final = step == STEPS
    return pl.pallas_call(
        functools.partial(absorb_step, step, final),
        out_shape=(HALF_STATE, HALF_STATE) if final else STATE,
        in_specs=[SMEM, SMEM, VMEM, VMEM, VMEM] + ([VMEM] if step else []),
        out_specs=(VMEM, VMEM) if final else VMEM,
        scratch_shapes=[pltpu.VMEM(STATE.shape, STATE.dtype)] if final else [],
        compiler_params=PARAMS,
        cost_estimate=pl.CostEstimate(flops=537_000_000, bytes_accessed=3_000_000, transcendentals=1_050_000),
        name="absorb",
    )(place, *planned, block, *([state] if step else []))


def call_merge(own, other):
    return pl.pallas_call(
        merge,
        out_shape=jax.ShapeDtypeStruct((ROWS, GROUP * HD), jnp.bfloat16),
        in_specs=[VMEM, VMEM],
        out_specs=VMEM,
        compiler_params=PARAMS,
        name="merge",
    )(own, other)


def at(xh, z, core):
    return (xh * Z + z) * CORE + core


def body(queries, span_keys, span_values, prefix_keys, prefix_values, span_seg, prefix_lengths):
    place = jnp.stack([lax.axis_index(a) for a in INST]).astype(jnp.int32)
    everyone = [(xh, z) for xh in range(XH) for z in range(Z)]
    cores = [(at(xh, z, c), at(xh, z, 1 - c)) for xh, z in everyone for c in range(CORE)]
    along = [(at(xh, z, c), at(xh, (z + 1 - 2 * c) % Z, c)) for xh, z in everyone for c in range(CORE)]

    span, pre = call_lay(span_keys, span_values, prefix_keys, prefix_values)
    pre = pre.reshape((XH * CORE * TP,) + pre.shape[2:])
    pre = lax.all_to_all(pre, ("xh", "core", "tp"), split_axis=0, concat_axis=0, tiled=True)
    span = lax.all_to_all(span, ("xh", "core"), split_axis=0, concat_axis=0, tiled=True)
    block = call_pack(span.reshape(XH * KEYS, 2 * HD), pre.reshape(XH * PIECE, 2 * HD))

    own_block, planned, state = block, None, None
    for step in range(1, STEPS + 1):
        leaving = block
        if step == STEPS:
            leaving = lax.dynamic_slice_in_dim(block, place[2] * HALF_ROWS, HALF_ROWS)
        arriving = lax.ppermute(leaving, INST, along)
        if step == 1:
            planned = call_plan(place, prefix_lengths, span_seg, queries, lax.ppermute(queries, INST, cores))
            block, planned = lax.optimization_barrier((arriving, planned))
            continue
        if step == 2:
            state = call_absorb(0, place, planned, own_block, state)
        state = call_absorb(step - 1, place, planned, block, state)
        block, state = lax.optimization_barrier((arriving, state))
    own, sib = call_absorb(STEPS, place, planned, block, state)
    return call_merge(own, lax.ppermute(sib, INST, cores))


def solution(mesh):
    cut = Mesh(mesh.devices.reshape(XH, Z, CORE, TP), INST + ("tp",))
    in_specs = (
        P(INST, "tp"),
        P(INST, "tp"),
        P(INST, "tp"),
        P(INST + ("tp",), None),
        P(INST + ("tp",), None),
        P(),
        P(),
    )
    return jax.shard_map(body, mesh=cut, in_specs=in_specs, out_specs=P(INST, "tp"), check_vma=False)
```

```python
import functools
import math

import jax
import jax.numpy as jnp
from jax import lax
from jax.experimental import pallas as pl
from jax.experimental.pallas import tpu as pltpu
from jax.sharding import Mesh, PartitionSpec as P

HEADS = 64
KV_HEADS = 8
HD = 128
GROUP = HEADS // KV_HEADS
REQ = 4
SPAN = 8192
PREFIX = 4096
XH, Z, CORE, TP = 2, 16, 2, 8
CHIPS = XH * Z
INST = ("xh", "z", "core")
ROWS = SPAN // (CHIPS * CORE)
KEYS = ROWS * CORE
PIECE = PREFIX // CHIPS
BLOCK_ROWS = KEYS + PIECE
LANES = 2 * ROWS
PARTS = GROUP * ROWS // LANES
STEPS = Z // 2
STATE_ROWS = HD + 8
LOW = -1e30
EXP2_SCALE = math.log2(math.e) / math.sqrt(HD)

SMEM = pl.BlockSpec(memory_space=pltpu.SMEM)
VMEM = pl.BlockSpec(memory_space=pltpu.VMEM)
PARAMS = pltpu.CompilerParams(vmem_limit_bytes=24 * 1024 * 1024)


def pack(place_ref, own_ref, sib_ref, across_ref, diagonal_ref, pre_ref, *block_refs):
    same_xh = [place_ref[0] == xh for xh in range(XH)]
    same_core = [place_ref[2] == core for core in range(CORE)]
    for xh in range(XH):
        for core in range(CORE):
            for i in range(2):
                near = jnp.where(same_core[core], own_ref[i], sib_ref[i])
                far = jnp.where(same_core[core], across_ref[i], diagonal_ref[i])
                block_refs[xh][core * ROWS : (core + 1) * ROWS, i * HD : (i + 1) * HD] = jnp.where(
                    same_xh[xh], near, far
                )
        block_refs[xh][KEYS:, :] = pre_ref[xh * PIECE : (xh + 1) * PIECE, :]


def plan(place_ref, lengths_ref, seg_ref, q_ref, sib_ref, scalars_ref, bounds_ref, rows_ref):
    inst = (place_ref[0] * Z + place_ref[1]) * CORE + place_ref[2]
    sibling = inst + 1 - 2 * place_ref[2]
    seg = seg_ref[...]
    counts = [jnp.int32(0)] + [
        jnp.sum(jnp.where(seg < s, 1.0, 0.0)).astype(jnp.int32) for s in range(1, REQ)
    ]
    starts, ends, running = [], [], jnp.int32(0)
    for s in range(REQ):
        starts.append(running)
        running = running + lengths_ref[s]
        ends.append(running)

    def pick(values, s):
        out = values[0]
        for k in range(1, REQ):
            out = jnp.where(s == k, values[k], out)
        return out

    for half, block in enumerate((inst, sibling)):
        first = block * ROWS
        first_seg, last_seg = jnp.int32(0), jnp.int32(0)
        for s in range(1, REQ):
            first_seg = first_seg + (first >= counts[s]).astype(jnp.int32)
            last_seg = last_seg + (first + ROWS - 1 >= counts[s]).astype(jnp.int32)
        values = (
            pick(starts, first_seg), pick(ends, last_seg), pick(starts, last_seg), pick(ends, first_seg),
            pick(counts, first_seg), first + ROWS, pick(counts, last_seg), first + 1,
        )
        for i, value in enumerate(values):
            scalars_ref[half * 8 + i] = value
        position = first + lax.broadcasted_iota(jnp.int32, (1, ROWS), 1)
        row_seg = jnp.zeros((1, ROWS), jnp.int32)
        for s in range(1, REQ):
            row_seg = row_seg + jnp.where(position >= counts[s], 1, 0)
        bounds_ref[half, 0:1, :] = pick(starts, row_seg)
        bounds_ref[half, 1:2, :] = pick(ends, row_seg)
        bounds_ref[half, 2:3, :] = pick(counts, row_seg)
        bounds_ref[half, 3:4, :] = position + 1
        ref = (q_ref, sib_ref)[half]
        for h in range(GROUP):
            rows_ref[half, h // 2, h % 2 * ROWS : (h % 2 + 1) * ROWS, :] = ref[:, h * HD : (h + 1) * HD]


def absorb_step(step, which, place_ref, scalars_ref, bounds_ref, rows_ref, block_ref, *refs):
    core, z = place_ref[2], place_ref[1]
    origin = lax.rem(jnp.where(core == 0, z - step + Z, z + step), Z)
    xh = core if which is None else which
    final = step == STEPS
    if final:
        _, state, own_ref, sib_ref = refs
    else:
        state = refs[-1]
    if step == 0:
        state[:, :, :HD, :] = jnp.zeros((CORE, PARTS, HD, LANES), jnp.float32)
        state[:, :, HD:, :] = jnp.zeros((CORE, PARTS, STATE_ROWS - HD, LANES), jnp.float32)
        state[:, :, HD : HD + 1, :] = jnp.full((CORE, PARTS, 1, LANES), LOW, jnp.float32)

    def absorb(half, row, count, base, kind, masked):
        keys = block_ref[row : row + count, :HD]
        vals = block_ref[row : row + count, HD:]
        if masked:
            index = base + lax.broadcasted_iota(jnp.int32, (count, ROWS), 0)
            low = bounds_ref[half, 2 * kind : 2 * kind + 1, :]
            high = bounds_ref[half, 2 * kind + 1 : 2 * kind + 2, :]
            bias = jnp.where((index >= low) & (index < high), 0.0, LOW)
            bias = jnp.concatenate([bias] * (LANES // ROWS), axis=1)
        for b in range(PARTS):
            scores = lax.dot_general(
                keys, rows_ref[half, b], (((1,), (1,)), ((), ())), preferred_element_type=jnp.float32
            )
            if masked:
                scores = scores + bias
            old = state[half, b, HD : HD + 1, :]
            new = jnp.maximum(old, jnp.max(scores, axis=0, keepdims=True))
            factor = jnp.exp2((old - new) * EXP2_SCALE)
            expo = jnp.exp2((scores - new) * EXP2_SCALE)
            total = state[half, b, HD + 1 : HD + 2, :] * factor + jnp.sum(expo, axis=0, keepdims=True)
            state[half, b, HD : HD + 1, :] = new
            state[half, b, HD + 1 : HD + 2, :] = total
            state[half, b, :HD, :] = state[half, b, :HD, :] * factor + lax.dot_general(
                vals, expo.astype(jnp.bfloat16), (((0,), (0,)), ((), ())), preferred_element_type=jnp.float32
            )

    def visit(half, row, count, base, kind):
        least_lo, most_hi, most_lo, least_hi = [scalars_ref[half * 8 + kind * 4 + i] for i in range(4)]
        seen = (base < most_hi) & (base + count > least_lo)
        whole = (base >= most_lo) & (base + count <= least_hi)

        @pl.when(seen & whole)
        def _():
            absorb(half, row, count, base, kind, False)

        @pl.when(seen & jnp.logical_not(whole))
        def _():
            absorb(half, row, count, base, kind, True)

    def one_half(half, carry):
        visit(half, 0, KEYS, (xh * Z + origin) * KEYS, 1)
        visit(half, KEYS, PIECE, (xh * Z + origin) * PIECE, 0)
        return carry

    lax.fori_loop(0, CORE, one_half, 0)
    if final:
        own_ref[...] = state[0]
        sib_ref[...] = state[1]


def merge(own_ref, other_ref, out_ref):
    for b in range(PARTS):
        top_a, top_b = own_ref[b, HD : HD + 1, :], other_ref[b, HD : HD + 1, :]
        top = jnp.maximum(top_a, top_b)
        factor_a = jnp.exp2((top_a - top) * EXP2_SCALE)
        factor_b = jnp.exp2((top_b - top) * EXP2_SCALE)
        total = own_ref[b, HD + 1 : HD + 2, :] * factor_a + other_ref[b, HD + 1 : HD + 2, :] * factor_b
        result = (own_ref[b, :HD, :] * factor_a + other_ref[b, :HD, :] * factor_b) / total
        for i in range(LANES // ROWS):
            h = b * (LANES // ROWS) + i
            out_ref[:, h * HD : (h + 1) * HD] = result[:, i * ROWS : (i + 1) * ROWS].T.astype(jnp.bfloat16)


STATE = jax.ShapeDtypeStruct((CORE, PARTS, STATE_ROWS, LANES), jnp.float32)
HALF_STATE = jax.ShapeDtypeStruct((PARTS, STATE_ROWS, LANES), jnp.float32)


def call_pack(place, *parts):
    return pl.pallas_call(
        pack,
        out_shape=(jax.ShapeDtypeStruct((BLOCK_ROWS, 2 * HD), jnp.bfloat16),) * XH,
        in_specs=[SMEM] + [VMEM] * 5,
        out_specs=(VMEM,) * XH,
        compiler_params=PARAMS,
        name="pack",
    )(place, *parts)


def call_plan(place, prefix_lengths, span_seg, queries, sib_queries):
    return pl.pallas_call(
        plan,
        out_shape=(
            jax.ShapeDtypeStruct((CORE * 8,), jnp.int32),
            jax.ShapeDtypeStruct((CORE, 8, ROWS), jnp.int32),
            jax.ShapeDtypeStruct((CORE, PARTS, LANES, HD), jnp.bfloat16),
        ),
        in_specs=[SMEM, SMEM, VMEM, VMEM, VMEM],
        out_specs=(SMEM, VMEM, VMEM),
        compiler_params=PARAMS,
        name="plan",
    )(place, prefix_lengths, span_seg.reshape(-1, ROWS), queries, sib_queries)


def call_absorb(step, which, place, planned, block, state):
    final = step == STEPS
    return pl.pallas_call(
        functools.partial(absorb_step, step, which),
        out_shape=(STATE, HALF_STATE, HALF_STATE) if final else STATE,
        in_specs=[SMEM, SMEM, VMEM, VMEM, VMEM] + ([VMEM] if step else []),
        out_specs=(VMEM,) * 3 if final else VMEM,
        input_output_aliases={5: 0} if step else {},
        compiler_params=PARAMS,
        cost_estimate=pl.CostEstimate(flops=400_000_000, bytes_accessed=2_000_000, transcendentals=790_000),
        name="absorb",
    )(place, *planned, block, *([state] if step else []))


def call_merge(own, other):
    return pl.pallas_call(
        merge,
        out_shape=jax.ShapeDtypeStruct((ROWS, GROUP * HD), jnp.bfloat16),
        in_specs=[VMEM, VMEM],
        out_specs=VMEM,
        compiler_params=PARAMS,
        name="merge",
    )(own, other)


def at(xh, z, core):
    return (xh * Z + z) * CORE + core


def body(queries, span_keys, span_values, prefix_keys, prefix_values, span_seg, prefix_lengths):
    place = jnp.stack([lax.axis_index(a) for a in INST]).astype(jnp.int32)
    everyone = [(xh, z, c) for xh in range(XH) for z in range(Z) for c in range(CORE)]
    sibling = [(at(xh, z, c), at(xh, z, 1 - c)) for xh, z, c in everyone]
    across = [(at(xh, z, c), at(1 - xh, z, c)) for xh, z, c in everyone]
    diagonal = [(at(xh, z, c), at(1 - xh, z, 1 - c)) for xh, z, c in everyone]
    along = [(at(xh, z, c), at(xh, (z + 1 - 2 * c) % Z, c)) for xh, z, c in everyone]

    pre = jnp.concatenate(
        [prefix_keys.reshape(-1, KV_HEADS, HD), prefix_values.reshape(-1, KV_HEADS, HD)], axis=2
    ).transpose(1, 0, 2)
    pre = jnp.broadcast_to(pre[None], (XH * CORE,) + pre.shape).reshape((XH * CORE * TP,) + pre.shape[1:])
    pre = lax.all_to_all(pre, ("xh", "core", "tp"), split_axis=0, concat_axis=0, tiled=True)
    pre = pre.reshape(XH * PIECE, 2 * HD)

    span = jnp.stack([span_keys, span_values])
    spans = [span] + [lax.ppermute(span, INST, way) for way in (sibling, across, diagonal)]
    blocks = list(call_pack(place, *spans, pre))
    planned = call_plan(place, prefix_lengths, span_seg, queries, lax.ppermute(queries, INST, sibling))

    mine = jnp.where(place[2] == 0, blocks[0], blocks[1])
    blocks = [lax.ppermute(block, INST, along) for block in blocks]
    state = call_absorb(0, None, place, planned, mine, None)
    for step in range(1, STEPS):
        for xh in range(XH):
            block, state = lax.optimization_barrier((blocks[xh], state))
            if step < STEPS - 1:
                blocks[xh] = lax.ppermute(block, INST, along)
            elif xh == 0:
                blocks[xh] = block
            else:
                mine = jnp.where(place[2] == 0, blocks[0], block)
                mine = lax.ppermute(mine, INST, along)
            state = call_absorb(step, xh, place, planned, block, state)
    _, own, sib = call_absorb(STEPS, None, place, planned, *lax.optimization_barrier((mine, state)))
    return call_merge(own, lax.ppermute(sib, INST, sibling))


def solution(mesh):
    cut = Mesh(mesh.devices.reshape(XH, Z, CORE, TP), INST + ("tp",))
    in_specs = (
        P(INST, "tp"),
        P(INST, "tp"),
        P(INST, "tp"),
        P(INST + ("tp",), None),
        P(INST + ("tp",), None),
        P(),
        P(),
    )
    return jax.shard_map(body, mesh=cut, in_specs=in_specs, out_specs=P(INST, "tp"), check_vma=False)
```

```python
import functools
import math

import jax
import jax.numpy as jnp
from jax import lax
from jax.experimental import pallas as pl
from jax.experimental.pallas import tpu as pltpu
from jax.sharding import Mesh, PartitionSpec as P

HEADS = 64
KV_HEADS = 8
HD = 128
GROUP = HEADS // KV_HEADS
REQ = 4
SPAN = 8192
PREFIX = 4096
XH, Z, CORE, TP = 2, 16, 2, 8
CHIPS = XH * Z
INST = ("xh", "z", "core")
ROWS = SPAN // (CHIPS * CORE)
KEYS = ROWS * CORE
PIECE = PREFIX // CHIPS
BLOCK_KEYS = KEYS + PIECE
LANES = 2 * ROWS
PARTS = GROUP * ROWS // LANES
STEPS = Z // 2
STATE_ROWS = HD + 8
LOW = -1e30
EXP2_SCALE = math.log2(math.e) / math.sqrt(HD)

SMEM = pl.BlockSpec(memory_space=pltpu.SMEM)
VMEM = pl.BlockSpec(memory_space=pltpu.VMEM)
PARAMS = pltpu.CompilerParams(vmem_limit_bytes=24 * 1024 * 1024)


def turn(tile):
    return tile.astype(jnp.float32).T.astype(jnp.bfloat16)


def pack(place_ref, own_ref, sib_ref, across_ref, diagonal_ref, pre_ref, *block_refs):
    same_xh = [place_ref[0] == xh for xh in range(XH)]
    same_core = [place_ref[2] == core for core in range(CORE)]
    for xh in range(XH):
        for core in range(CORE):
            tiles = []
            for i in range(2):
                near = jnp.where(same_core[core], own_ref[i], sib_ref[i])
                far = jnp.where(same_core[core], across_ref[i], diagonal_ref[i])
                tiles.append(jnp.where(same_xh[xh], near, far))
            block_refs[xh][core * ROWS : (core + 1) * ROWS, :] = tiles[0]
            block_refs[xh][BLOCK_KEYS + core * HD : BLOCK_KEYS + (core + 1) * HD, :] = turn(tiles[1])
        block_refs[xh][KEYS:BLOCK_KEYS, :] = pre_ref[xh * PIECE : (xh + 1) * PIECE, :HD]
        block_refs[xh][BLOCK_KEYS + KEYS :, :] = turn(pre_ref[xh * PIECE : (xh + 1) * PIECE, HD:])


def plan(place_ref, lengths_ref, seg_ref, q_ref, sib_ref, scalars_ref, bounds_ref, rows_ref):
    inst = (place_ref[0] * Z + place_ref[1]) * CORE + place_ref[2]
    sibling = inst + 1 - 2 * place_ref[2]
    seg = seg_ref[...]
    counts = [jnp.int32(0)] + [
        jnp.sum(jnp.where(seg < s, 1.0, 0.0)).astype(jnp.int32) for s in range(1, REQ)
    ]
    starts, ends, running = [], [], jnp.int32(0)
    for s in range(REQ):
        starts.append(running)
        running = running + lengths_ref[s]
        ends.append(running)

    def pick(values, s):
        out = values[0]
        for k in range(1, REQ):
            out = jnp.where(s == k, values[k], out)
        return out

    for half, block in enumerate((inst, sibling)):
        first = block * ROWS
        first_seg, last_seg = jnp.int32(0), jnp.int32(0)
        for s in range(1, REQ):
            first_seg = first_seg + (first >= counts[s]).astype(jnp.int32)
            last_seg = last_seg + (first + ROWS - 1 >= counts[s]).astype(jnp.int32)
        values = (
            pick(starts, first_seg), pick(ends, last_seg), pick(starts, last_seg), pick(ends, first_seg),
            pick(counts, first_seg), first + ROWS, pick(counts, last_seg), first + 1,
        )
        for i, value in enumerate(values):
            scalars_ref[half * 8 + i] = value
        position = first + lax.broadcasted_iota(jnp.int32, (1, ROWS), 1)
        row_seg = jnp.zeros((1, ROWS), jnp.int32)
        for s in range(1, REQ):
            row_seg = row_seg + jnp.where(position >= counts[s], 1, 0)
        bounds_ref[half, 0:1, :] = pick(starts, row_seg)
        bounds_ref[half, 1:2, :] = pick(ends, row_seg)
        bounds_ref[half, 2:3, :] = pick(counts, row_seg)
        bounds_ref[half, 3:4, :] = position + 1
        ref = (q_ref, sib_ref)[half]
        for h in range(GROUP):
            rows_ref[half, h // 2, :, h % 2 * ROWS : (h % 2 + 1) * ROWS] = turn(ref[:, h * HD : (h + 1) * HD])


def absorb_step(step, which, place_ref, scalars_ref, bounds_ref, rows_ref, block_ref, *refs):
    core, z = place_ref[2], place_ref[1]
    origin = lax.rem(jnp.where(core == 0, z - step + Z, z + step), Z)
    xh = core if which is None else which
    final = step == STEPS
    if final:
        _, state, own_ref, sib_ref = refs
    else:
        state = refs[-1]
    if step == 0:
        state[:, :, :HD, :] = jnp.zeros((CORE, PARTS, HD, LANES), jnp.float32)
        state[:, :, HD:, :] = jnp.zeros((CORE, PARTS, STATE_ROWS - HD, LANES), jnp.float32)
        state[:, :, HD : HD + 1, :] = jnp.full((CORE, PARTS, 1, LANES), LOW, jnp.float32)

    def absorb(half, row, count, base, kind, masked):
        keys = block_ref[row : row + count, :]
        vals = jnp.concatenate(
            [block_ref[BLOCK_KEYS + i : BLOCK_KEYS + i + HD, :] for i in range(row, row + count, HD)], axis=1
        )
        every = range(PARTS)
        scores = [jnp.dot(keys, rows_ref[half, b], preferred_element_type=jnp.float32) for b in every]
        if masked:
            index = base + lax.broadcasted_iota(jnp.int32, (count, ROWS), 0)
            low = bounds_ref[half, 2 * kind : 2 * kind + 1, :]
            high = bounds_ref[half, 2 * kind + 1 : 2 * kind + 2, :]
            bias = jnp.where((index >= low) & (index < high), 0.0, LOW)
            bias = jnp.concatenate([bias] * (LANES // ROWS), axis=1)
            scores = [scores[b] + bias for b in every]
        old = [state[half, b, HD : HD + 1, :] for b in every]
        new = [jnp.maximum(old[b], jnp.max(scores[b], axis=0, keepdims=True)) for b in every]
        factor = [jnp.exp2((old[b] - new[b]) * EXP2_SCALE) for b in every]
        expo = [jnp.exp2((scores[b] - new[b]) * EXP2_SCALE) for b in every]
        total = [
            state[half, b, HD + 1 : HD + 2, :] * factor[b] + jnp.sum(expo[b], axis=0, keepdims=True) for b in every
        ]
        summed = [
            state[half, b, :HD, :] * factor[b]
            + jnp.dot(vals, expo[b].astype(jnp.bfloat16), preferred_element_type=jnp.float32)
            for b in every
        ]
        for b in every:
            state[half, b, :HD, :] = summed[b]
            state[half, b, HD : HD + 1, :] = new[b]
            state[half, b, HD + 1 : HD + 2, :] = total[b]

    def visit(half, row, count, base, kind):
        least_lo, most_hi, most_lo, least_hi = [scalars_ref[half * 8 + kind * 4 + i] for i in range(4)]
        seen = (base < most_hi) & (base + count > least_lo)
        whole = (base >= most_lo) & (base + count <= least_hi)

        @pl.when(seen & whole)
        def _():
            absorb(half, row, count, base, kind, False)

        @pl.when(seen & jnp.logical_not(whole))
        def _():
            absorb(half, row, count, base, kind, True)

    def one_half(half, carry):
        visit(half, 0, KEYS, (xh * Z + origin) * KEYS, 1)
        visit(half, KEYS, PIECE, (xh * Z + origin) * PIECE, 0)
        return carry

    lax.fori_loop(0, CORE, one_half, 0)
    if final:
        own_ref[...] = state[0]
        sib_ref[...] = state[1]


def merge(own_ref, other_ref, out_ref):
    for b in range(PARTS):
        top_a, top_b = own_ref[b, HD : HD + 1, :], other_ref[b, HD : HD + 1, :]
        top = jnp.maximum(top_a, top_b)
        factor_a = jnp.exp2((top_a - top) * EXP2_SCALE)
        factor_b = jnp.exp2((top_b - top) * EXP2_SCALE)
        total = own_ref[b, HD + 1 : HD + 2, :] * factor_a + other_ref[b, HD + 1 : HD + 2, :] * factor_b
        result = (own_ref[b, :HD, :] * factor_a + other_ref[b, :HD, :] * factor_b) / total
        for i in range(LANES // ROWS):
            h = b * (LANES // ROWS) + i
            out_ref[:, h * HD : (h + 1) * HD] = result[:, i * ROWS : (i + 1) * ROWS].T.astype(jnp.bfloat16)


STATE = jax.ShapeDtypeStruct((CORE, PARTS, STATE_ROWS, LANES), jnp.float32)
HALF_STATE = jax.ShapeDtypeStruct((PARTS, STATE_ROWS, LANES), jnp.float32)


def call_pack(place, *parts):
    return pl.pallas_call(
        pack,
        out_shape=(jax.ShapeDtypeStruct((2 * BLOCK_KEYS, HD), jnp.bfloat16),) * XH,
        in_specs=[SMEM] + [VMEM] * 5,
        out_specs=(VMEM,) * XH,
        compiler_params=PARAMS,
        name="pack",
    )(place, *parts)


def call_plan(place, prefix_lengths, span_seg, queries, sib_queries):
    return pl.pallas_call(
        plan,
        out_shape=(
            jax.ShapeDtypeStruct((CORE * 8,), jnp.int32),
            jax.ShapeDtypeStruct((CORE, 8, ROWS), jnp.int32),
            jax.ShapeDtypeStruct((CORE, PARTS, HD, LANES), jnp.bfloat16),
        ),
        in_specs=[SMEM, SMEM, VMEM, VMEM, VMEM],
        out_specs=(SMEM, VMEM, VMEM),
        compiler_params=PARAMS,
        name="plan",
    )(place, prefix_lengths, span_seg.reshape(-1, ROWS), queries, sib_queries)


def call_absorb(step, which, place, planned, block, state):
    final = step == STEPS
    return pl.pallas_call(
        functools.partial(absorb_step, step, which),
        out_shape=(STATE, HALF_STATE, HALF_STATE) if final else STATE,
        in_specs=[SMEM, SMEM, VMEM, VMEM, VMEM] + ([VMEM] if step else []),
        out_specs=(VMEM,) * 3 if final else VMEM,
        input_output_aliases={5: 0} if step else {},
        compiler_params=PARAMS,
        cost_estimate=pl.CostEstimate(flops=400_000_000, bytes_accessed=2_000_000, transcendentals=790_000),
        name="absorb",
    )(place, *planned, block, *([state] if step else []))


def call_merge(own, other):
    return pl.pallas_call(
        merge,
        out_shape=jax.ShapeDtypeStruct((ROWS, GROUP * HD), jnp.bfloat16),
        in_specs=[VMEM, VMEM],
        out_specs=VMEM,
        compiler_params=PARAMS,
        name="merge",
    )(own, other)


def at(xh, z, core):
    return (xh * Z + z) * CORE + core


def body(queries, span_keys, span_values, prefix_keys, prefix_values, span_seg, prefix_lengths):
    place = jnp.stack([lax.axis_index(a) for a in INST]).astype(jnp.int32)
    everyone = [(xh, z, c) for xh in range(XH) for z in range(Z) for c in range(CORE)]
    sibling = [(at(xh, z, c), at(xh, z, 1 - c)) for xh, z, c in everyone]
    across = [(at(xh, z, c), at(1 - xh, z, c)) for xh, z, c in everyone]
    diagonal = [(at(xh, z, c), at(1 - xh, z, 1 - c)) for xh, z, c in everyone]
    along = [(at(xh, z, c), at(xh, (z + 1 - 2 * c) % Z, c)) for xh, z, c in everyone]

    pre = jnp.concatenate(
        [prefix_keys.reshape(-1, KV_HEADS, HD), prefix_values.reshape(-1, KV_HEADS, HD)], axis=2
    ).transpose(1, 0, 2)
    pre = jnp.broadcast_to(pre[None], (XH * CORE,) + pre.shape).reshape((XH * CORE * TP,) + pre.shape[1:])
    pre = lax.all_to_all(pre, ("xh", "core", "tp"), split_axis=0, concat_axis=0, tiled=True)
    pre = pre.reshape(XH * PIECE, 2 * HD)

    span = jnp.stack([span_keys, span_values])
    spans = [span] + [lax.ppermute(span, INST, way) for way in (sibling, across, diagonal)]
    blocks = list(call_pack(place, *spans, pre))
    planned = call_plan(place, prefix_lengths, span_seg, queries, lax.ppermute(queries, INST, sibling))

    mine = jnp.where(place[2] == 0, blocks[0], blocks[1])
    blocks = [lax.ppermute(block, INST, along) for block in blocks]
    state = call_absorb(0, None, place, planned, mine, None)
    for step in range(1, STEPS):
        for xh in range(XH):
            block, state = lax.optimization_barrier((blocks[xh], state))
            if step < STEPS - 1:
                blocks[xh] = lax.ppermute(block, INST, along)
            elif xh == 0:
                blocks[xh] = block
            else:
                mine = jnp.where(place[2] == 0, blocks[0], block)
                mine = lax.ppermute(mine, INST, along)
            state = call_absorb(step, xh, place, planned, block, state)
    _, own, sib = call_absorb(STEPS, None, place, planned, *lax.optimization_barrier((mine, state)))
    return call_merge(own, lax.ppermute(sib, INST, sibling))


def solution(mesh):
    cut = Mesh(mesh.devices.reshape(XH, Z, CORE, TP), INST + ("tp",))
    in_specs = (
        P(INST, "tp"),
        P(INST, "tp"),
        P(INST, "tp"),
        P(INST + ("tp",), None),
        P(INST + ("tp",), None),
        P(),
        P(),
    )
    return jax.shard_map(body, mesh=cut, in_specs=in_specs, out_specs=P(INST, "tp"), check_vma=False)
```

```python
import functools
import math

import jax
import jax.numpy as jnp
from jax import lax
from jax.experimental import pallas as pl
from jax.experimental.pallas import tpu as pltpu
from jax.sharding import Mesh, PartitionSpec as P

HEADS = 64
KV_HEADS = 8
HD = 128
GROUP = HEADS // KV_HEADS
REQ = 4
SPAN = 8192
PREFIX = 4096
XH, Z, CORE, TP = 2, 16, 2, 8
CHIPS = XH * Z
INST = ("xh", "z", "core")
ROWS = SPAN // (CHIPS * CORE)
KEYS = ROWS * CORE
PIECE = PREFIX // CHIPS
BLOCK_KEYS = KEYS + PIECE
LANES = 2 * ROWS
PARTS = GROUP * ROWS // LANES
STEPS = Z // 2
STATE_ROWS = HD + 8
LOW = -1e30
EXP2_SCALE = math.log2(math.e) / math.sqrt(HD)

SMEM = pl.BlockSpec(memory_space=pltpu.SMEM)
VMEM = pl.BlockSpec(memory_space=pltpu.VMEM)
PARAMS = pltpu.CompilerParams(vmem_limit_bytes=24 * 1024 * 1024)


def turn(tile):
    return tile.astype(jnp.float32).T.astype(jnp.bfloat16)


def pack(place_ref, own_ref, sib_ref, across_ref, diagonal_ref, pre_ref, *block_refs):
    same_xh = [place_ref[0] == xh for xh in range(XH)]
    same_core = [place_ref[2] == core for core in range(CORE)]
    for xh in range(XH):
        for core in range(CORE):
            tiles = []
            for i in range(2):
                near = jnp.where(same_core[core], own_ref[i], sib_ref[i])
                far = jnp.where(same_core[core], across_ref[i], diagonal_ref[i])
                tiles.append(jnp.where(same_xh[xh], near, far))
            block_refs[xh][core * ROWS : (core + 1) * ROWS, :] = tiles[0]
            block_refs[xh][BLOCK_KEYS + core * HD : BLOCK_KEYS + (core + 1) * HD, :] = turn(tiles[1])
        block_refs[xh][KEYS:BLOCK_KEYS, :] = pre_ref[xh * PIECE : (xh + 1) * PIECE, :HD]
        block_refs[xh][BLOCK_KEYS + KEYS :, :] = turn(pre_ref[xh * PIECE : (xh + 1) * PIECE, HD:])


def plan(place_ref, lengths_ref, seg_ref, q_ref, sib_ref, scalars_ref, bounds_ref, rows_ref):
    inst = (place_ref[0] * Z + place_ref[1]) * CORE + place_ref[2]
    sibling = inst + 1 - 2 * place_ref[2]
    seg = seg_ref[...]
    counts = [jnp.int32(0)] + [
        jnp.sum(jnp.where(seg < s, 1.0, 0.0)).astype(jnp.int32) for s in range(1, REQ)
    ]
    starts, ends, running = [], [], jnp.int32(0)
    for s in range(REQ):
        starts.append(running)
        running = running + lengths_ref[s]
        ends.append(running)

    def pick(values, s):
        out = values[0]
        for k in range(1, REQ):
            out = jnp.where(s == k, values[k], out)
        return out

    for half, block in enumerate((inst, sibling)):
        first = block * ROWS
        first_seg, last_seg = jnp.int32(0), jnp.int32(0)
        for s in range(1, REQ):
            first_seg = first_seg + (first >= counts[s]).astype(jnp.int32)
            last_seg = last_seg + (first + ROWS - 1 >= counts[s]).astype(jnp.int32)
        values = (
            pick(starts, first_seg), pick(ends, last_seg), pick(starts, last_seg), pick(ends, first_seg),
            pick(counts, first_seg), first + ROWS, pick(counts, last_seg), first + 1,
        )
        for i, value in enumerate(values):
            scalars_ref[half * 8 + i] = value
        position = first + lax.broadcasted_iota(jnp.int32, (1, ROWS), 1)
        row_seg = jnp.zeros((1, ROWS), jnp.int32)
        for s in range(1, REQ):
            row_seg = row_seg + jnp.where(position >= counts[s], 1, 0)
        bounds_ref[half, 0:1, :] = pick(starts, row_seg)
        bounds_ref[half, 1:2, :] = pick(ends, row_seg)
        bounds_ref[half, 2:3, :] = pick(counts, row_seg)
        bounds_ref[half, 3:4, :] = position + 1
        ref = (q_ref, sib_ref)[half]
        for h in range(GROUP):
            rows_ref[half, h // 2, :, h % 2 * ROWS : (h % 2 + 1) * ROWS] = turn(ref[:, h * HD : (h + 1) * HD])


def absorb_step(step, which, final, place_ref, scalars_ref, bounds_ref, rows_ref, block_ref, *refs):
    core, z = place_ref[2], place_ref[1]
    origin = lax.rem(jnp.where(core == 0, z - step + Z, z + step), Z)
    xh = core if which is None else which
    if final:
        _, state, own_ref, sib_ref = refs
    else:
        state = refs[-1]
    if step == 0:
        state[:, :, :HD, :] = jnp.zeros((CORE, PARTS, HD, LANES), jnp.float32)
        state[:, :, HD:, :] = jnp.zeros((CORE, PARTS, STATE_ROWS - HD, LANES), jnp.float32)
        state[:, :, HD : HD + 1, :] = jnp.full((CORE, PARTS, 1, LANES), LOW, jnp.float32)

    def absorb(half, row, count, base, kind, masked):
        keys = block_ref[row : row + count, :]
        vals = jnp.concatenate(
            [block_ref[BLOCK_KEYS + i : BLOCK_KEYS + i + HD, :] for i in range(row, row + count, HD)], axis=1
        )
        every = range(PARTS)
        scores = [jnp.dot(keys, rows_ref[half, b], preferred_element_type=jnp.float32) for b in every]
        if masked:
            index = base + lax.broadcasted_iota(jnp.int32, (count, ROWS), 0)
            low = bounds_ref[half, 2 * kind : 2 * kind + 1, :]
            high = bounds_ref[half, 2 * kind + 1 : 2 * kind + 2, :]
            bias = jnp.where((index >= low) & (index < high), 0.0, LOW)
            bias = jnp.concatenate([bias] * (LANES // ROWS), axis=1)
            scores = [scores[b] + bias for b in every]
        old = [state[half, b, HD : HD + 1, :] for b in every]
        new = [jnp.maximum(old[b], jnp.max(scores[b], axis=0, keepdims=True)) for b in every]
        factor = [jnp.exp2((old[b] - new[b]) * EXP2_SCALE) for b in every]
        expo = [jnp.exp2((scores[b] - new[b]) * EXP2_SCALE) for b in every]
        total = [
            state[half, b, HD + 1 : HD + 2, :] * factor[b] + jnp.sum(expo[b], axis=0, keepdims=True) for b in every
        ]
        summed = [
            state[half, b, :HD, :] * factor[b]
            + jnp.dot(vals, expo[b].astype(jnp.bfloat16), preferred_element_type=jnp.float32)
            for b in every
        ]
        for b in every:
            state[half, b, :HD, :] = summed[b]
            state[half, b, HD : HD + 1, :] = new[b]
            state[half, b, HD + 1 : HD + 2, :] = total[b]

    def visit(half, row, count, base, kind):
        least_lo, most_hi, most_lo, least_hi = [scalars_ref[half * 8 + kind * 4 + i] for i in range(4)]
        seen = (base < most_hi) & (base + count > least_lo)
        if step == STEPS:
            seen = seen & (core == 1)
        whole = (base >= most_lo) & (base + count <= least_hi)

        @pl.when(seen & whole)
        def _():
            absorb(half, row, count, base, kind, False)

        @pl.when(seen & jnp.logical_not(whole))
        def _():
            absorb(half, row, count, base, kind, True)

    def one_half(half, carry):
        visit(half, 0, KEYS, (xh * Z + origin) * KEYS, 1)
        visit(half, KEYS, PIECE, (xh * Z + origin) * PIECE, 0)
        return carry

    lax.fori_loop(0, CORE, one_half, 0)
    if final:
        own_ref[...] = state[0]
        sib_ref[...] = state[1]


def merge(own_ref, other_ref, out_ref):
    for b in range(PARTS):
        top_a, top_b = own_ref[b, HD : HD + 1, :], other_ref[b, HD : HD + 1, :]
        top = jnp.maximum(top_a, top_b)
        factor_a = jnp.exp2((top_a - top) * EXP2_SCALE)
        factor_b = jnp.exp2((top_b - top) * EXP2_SCALE)
        total = own_ref[b, HD + 1 : HD + 2, :] * factor_a + other_ref[b, HD + 1 : HD + 2, :] * factor_b
        result = (own_ref[b, :HD, :] * factor_a + other_ref[b, :HD, :] * factor_b) / total
        for i in range(LANES // ROWS):
            h = b * (LANES // ROWS) + i
            out_ref[:, h * HD : (h + 1) * HD] = result[:, i * ROWS : (i + 1) * ROWS].T.astype(jnp.bfloat16)


STATE = jax.ShapeDtypeStruct((CORE, PARTS, STATE_ROWS, LANES), jnp.float32)
HALF_STATE = jax.ShapeDtypeStruct((PARTS, STATE_ROWS, LANES), jnp.float32)


def call_pack(place, *parts):
    return pl.pallas_call(
        pack,
        out_shape=(jax.ShapeDtypeStruct((2 * BLOCK_KEYS, HD), jnp.bfloat16),) * XH,
        in_specs=[SMEM] + [VMEM] * 5,
        out_specs=(VMEM,) * XH,
        compiler_params=PARAMS,
        name="pack",
    )(place, *parts)


def call_plan(place, prefix_lengths, span_seg, queries, sib_queries):
    return pl.pallas_call(
        plan,
        out_shape=(
            jax.ShapeDtypeStruct((CORE * 8,), jnp.int32),
            jax.ShapeDtypeStruct((CORE, 8, ROWS), jnp.int32),
            jax.ShapeDtypeStruct((CORE, PARTS, HD, LANES), jnp.bfloat16),
        ),
        in_specs=[SMEM, SMEM, VMEM, VMEM, VMEM],
        out_specs=(SMEM, VMEM, VMEM),
        compiler_params=PARAMS,
        name="plan",
    )(place, prefix_lengths, span_seg.reshape(-1, ROWS), queries, sib_queries)


def call_absorb(step, which, place, planned, block, state):
    final = step == STEPS and which == XH - 1
    return pl.pallas_call(
        functools.partial(absorb_step, step, which, final),
        out_shape=(STATE, HALF_STATE, HALF_STATE) if final else STATE,
        in_specs=[SMEM, SMEM, VMEM, VMEM, VMEM] + ([VMEM] if step else []),
        out_specs=(VMEM,) * 3 if final else VMEM,
        input_output_aliases={5: 0} if step else {},
        compiler_params=PARAMS,
        cost_estimate=pl.CostEstimate(flops=400_000_000, bytes_accessed=2_000_000, transcendentals=790_000),
        name="absorb",
    )(place, *planned, block, *([state] if step else []))


def call_merge(own, other):
    return pl.pallas_call(
        merge,
        out_shape=jax.ShapeDtypeStruct((ROWS, GROUP * HD), jnp.bfloat16),
        in_specs=[VMEM, VMEM],
        out_specs=VMEM,
        compiler_params=PARAMS,
        name="merge",
    )(own, other)


def at(xh, z, core):
    return (xh * Z + z) * CORE + core


def body(queries, span_keys, span_values, prefix_keys, prefix_values, span_seg, prefix_lengths):
    place = jnp.stack([lax.axis_index(a) for a in INST]).astype(jnp.int32)
    everyone = [(xh, z, c) for xh in range(XH) for z in range(Z) for c in range(CORE)]
    sibling = [(at(xh, z, c), at(xh, z, 1 - c)) for xh, z, c in everyone]
    across = [(at(xh, z, c), at(1 - xh, z, c)) for xh, z, c in everyone]
    diagonal = [(at(xh, z, c), at(1 - xh, z, 1 - c)) for xh, z, c in everyone]
    along = [(at(xh, z, c), at(xh, (z + 1 - 2 * c) % Z, c)) for xh, z, c in everyone]
    down = [way for way in along if way[0] % CORE == 1]

    pre = jnp.concatenate(
        [prefix_keys.reshape(-1, KV_HEADS, HD), prefix_values.reshape(-1, KV_HEADS, HD)], axis=2
    ).transpose(1, 0, 2)
    pre = jnp.broadcast_to(pre[None], (XH * CORE,) + pre.shape).reshape((XH * CORE * TP,) + pre.shape[1:])
    pre = lax.all_to_all(pre, ("xh", "core", "tp"), split_axis=0, concat_axis=0, tiled=True)
    pre = pre.reshape(XH * PIECE, 2 * HD)

    span = jnp.stack([span_keys, span_values])
    spans = [span] + [lax.ppermute(span, INST, way) for way in (sibling, across, diagonal)]
    blocks = list(call_pack(place, *spans, pre))
    planned = call_plan(place, prefix_lengths, span_seg, queries, lax.ppermute(queries, INST, sibling))

    mine = jnp.where(place[2] == 0, blocks[0], blocks[1])
    blocks = [lax.ppermute(block, INST, along) for block in blocks]
    state = call_absorb(0, None, place, planned, mine, None)
    for step in range(1, STEPS + 1):
        for xh in range(XH):
            block, state = lax.optimization_barrier((blocks[xh], state))
            if step < STEPS:
                blocks[xh] = lax.ppermute(block, INST, along if step < STEPS - 1 else down)
            state = call_absorb(step, xh, place, planned, block, state)
    _, own, sib = state
    return call_merge(own, lax.ppermute(sib, INST, sibling))


def solution(mesh):
    cut = Mesh(mesh.devices.reshape(XH, Z, CORE, TP), INST + ("tp",))
    in_specs = (
        P(INST, "tp"),
        P(INST, "tp"),
        P(INST, "tp"),
        P(INST + ("tp",), None),
        P(INST + ("tp",), None),
        P(),
        P(),
    )
    return jax.shard_map(body, mesh=cut, in_specs=in_specs, out_specs=P(INST, "tp"), check_vma=False)
```

```python
import functools
import math

import jax
import jax.numpy as jnp
from jax import lax
from jax.experimental import pallas as pl
from jax.experimental.pallas import tpu as pltpu
from jax.sharding import Mesh, PartitionSpec as P

HEADS = 64
KV_HEADS = 8
HD = 128
GROUP = HEADS // KV_HEADS
REQ = 4
SPAN = 8192
PREFIX = 4096
XH, Z, CORE, TP = 2, 16, 2, 8
CHIPS = XH * Z
INST = ("xh", "z", "core")
ROWS = SPAN // (CHIPS * CORE)
KEYS = ROWS * XH
PIECE = PREFIX // (CHIPS * CORE)
BLOCK_KEYS = KEYS + XH * PIECE
LANES = 2 * ROWS
PARTS = GROUP * ROWS // LANES
STEPS = Z // 2
STATE_ROWS = HD + 8
LOW = -1e30
EXP2_SCALE = math.log2(math.e) / math.sqrt(HD)

SMEM = pl.BlockSpec(memory_space=pltpu.SMEM)
VMEM = pl.BlockSpec(memory_space=pltpu.VMEM)
PARAMS = pltpu.CompilerParams(vmem_limit_bytes=24 * 1024 * 1024)


def turn(tile):
    return tile.astype(jnp.float32).T.astype(jnp.bfloat16)


def pack(place_ref, own_ref, across_ref, pre_ref, block_ref):
    for xh in range(XH):
        tiles = [jnp.where(place_ref[0] == xh, own_ref[i], across_ref[i]) for i in range(2)]
        block_ref[xh * ROWS : (xh + 1) * ROWS, :] = tiles[0]
        block_ref[BLOCK_KEYS + xh * HD : BLOCK_KEYS + (xh + 1) * HD, :] = turn(tiles[1])
    block_ref[KEYS:BLOCK_KEYS, :] = pre_ref[:, :HD]
    block_ref[BLOCK_KEYS + KEYS :, :] = turn(pre_ref[:, HD:])


def plan(place_ref, lengths_ref, seg_ref, q_ref, sib_ref, scalars_ref, bounds_ref, rows_ref):
    inst = (place_ref[0] * Z + place_ref[1]) * CORE + place_ref[2]
    sibling = inst + 1 - 2 * place_ref[2]
    seg = seg_ref[...]
    counts = [jnp.int32(0)] + [
        jnp.sum(jnp.where(seg < s, 1.0, 0.0)).astype(jnp.int32) for s in range(1, REQ)
    ]
    starts, ends, running = [], [], jnp.int32(0)
    for s in range(REQ):
        starts.append(running)
        running = running + lengths_ref[s]
        ends.append(running)

    def pick(values, s):
        out = values[0]
        for k in range(1, REQ):
            out = jnp.where(s == k, values[k], out)
        return out

    for half, block in enumerate((inst, sibling)):
        first = block * ROWS
        first_seg, last_seg = jnp.int32(0), jnp.int32(0)
        for s in range(1, REQ):
            first_seg = first_seg + (first >= counts[s]).astype(jnp.int32)
            last_seg = last_seg + (first + ROWS - 1 >= counts[s]).astype(jnp.int32)
        values = (
            pick(starts, first_seg), pick(ends, last_seg), pick(starts, last_seg), pick(ends, first_seg),
            pick(counts, first_seg), first + ROWS, pick(counts, last_seg), first + 1,
        )
        for i, value in enumerate(values):
            scalars_ref[half * 8 + i] = value
        position = first + lax.broadcasted_iota(jnp.int32, (1, ROWS), 1)
        row_seg = jnp.zeros((1, ROWS), jnp.int32)
        for s in range(1, REQ):
            row_seg = row_seg + jnp.where(position >= counts[s], 1, 0)
        bounds_ref[half, 0:1, :] = pick(starts, row_seg)
        bounds_ref[half, 1:2, :] = pick(ends, row_seg)
        bounds_ref[half, 2:3, :] = pick(counts, row_seg)
        bounds_ref[half, 3:4, :] = position + 1
        ref = (q_ref, sib_ref)[half]
        for h in range(GROUP):
            rows_ref[half, h // 2, :, h % 2 * ROWS : (h % 2 + 1) * ROWS] = turn(ref[:, h * HD : (h + 1) * HD])


def absorb_step(step, turned, final, place_ref, scalars_ref, bounds_ref, rows_ref, block_ref, *refs):
    core, z = place_ref[2], place_ref[1]
    upward = (core == 1) if turned else (core == 0)
    origin = lax.rem(jnp.where(upward, z - step + Z, z + step), Z)
    if final:
        _, state, own_ref, sib_ref = refs
    else:
        state = refs[-1]
    if step == 0:
        state[:, :, :HD, :] = jnp.zeros((CORE, PARTS, HD, LANES), jnp.float32)
        state[:, :, HD:, :] = jnp.zeros((CORE, PARTS, STATE_ROWS - HD, LANES), jnp.float32)
        state[:, :, HD : HD + 1, :] = jnp.full((CORE, PARTS, 1, LANES), LOW, jnp.float32)

    def absorb(half, row, count, index, kind, masked):
        keys = block_ref[row : row + count, :]
        vals = jnp.concatenate(
            [block_ref[BLOCK_KEYS + i : BLOCK_KEYS + i + HD, :] for i in range(row, row + count, HD)], axis=1
        )
        every = range(PARTS)
        scores = [jnp.dot(keys, rows_ref[half, b], preferred_element_type=jnp.float32) for b in every]
        if masked:
            low = bounds_ref[half, 2 * kind : 2 * kind + 1, :]
            high = bounds_ref[half, 2 * kind + 1 : 2 * kind + 2, :]
            bias = jnp.where((index >= low) & (index < high), 0.0, LOW)
            bias = jnp.concatenate([bias] * (LANES // ROWS), axis=1)
            scores = [scores[b] + bias for b in every]
        old = [state[half, b, HD : HD + 1, :] for b in every]
        new = [jnp.maximum(old[b], jnp.max(scores[b], axis=0, keepdims=True)) for b in every]
        factor = [jnp.exp2((old[b] - new[b]) * EXP2_SCALE) for b in every]
        expo = [jnp.exp2((scores[b] - new[b]) * EXP2_SCALE) for b in every]
        total = [
            state[half, b, HD + 1 : HD + 2, :] * factor[b] + jnp.sum(expo[b], axis=0, keepdims=True) for b in every
        ]
        summed = [
            state[half, b, :HD, :] * factor[b]
            + jnp.dot(vals, expo[b].astype(jnp.bfloat16), preferred_element_type=jnp.float32)
            for b in every
        ]
        for b in every:
            state[half, b, :HD, :] = summed[b]
            state[half, b, HD : HD + 1, :] = new[b]
            state[half, b, HD + 1 : HD + 2, :] = total[b]

    def overlaps(half, base, count, kind):
        return (base < scalars_ref[half * 8 + kind * 4 + 1]) & (base + count > scalars_ref[half * 8 + kind * 4])

    offset = lax.broadcasted_iota(jnp.int32, (ROWS, ROWS), 0)

    def one_half(half, carry):
        for xh in range(XH):
            base = ((xh * Z + origin) * CORE + core) * ROWS
            seen = overlaps(half, base, ROWS, 1)
            whole = (base >= scalars_ref[half * 8 + 6]) & (base + ROWS <= scalars_ref[half * 8 + 7])

            @pl.when(seen & whole)
            def _():
                absorb(half, xh * ROWS, ROWS, None, 1, False)

            @pl.when(seen & jnp.logical_not(whole))
            def _():
                absorb(half, xh * ROWS, ROWS, base + offset, 1, True)

        base = (origin * CORE + core) * PIECE
        apart = PREFIX // XH

        @pl.when(overlaps(half, base, PIECE, 0) | overlaps(half, base + apart, PIECE, 0))
        def _():
            absorb(half, KEYS, XH * PIECE, base + offset + jnp.where(offset >= PIECE, apart - PIECE, 0), 0, True)

        return carry

    lax.fori_loop(0, CORE, one_half, 0)
    if final:
        own_ref[...] = state[0]
        sib_ref[...] = state[1]


def merge(own_ref, other_ref, out_ref):
    for b in range(PARTS):
        top_a, top_b = own_ref[b, HD : HD + 1, :], other_ref[b, HD : HD + 1, :]
        top = jnp.maximum(top_a, top_b)
        factor_a = jnp.exp2((top_a - top) * EXP2_SCALE)
        factor_b = jnp.exp2((top_b - top) * EXP2_SCALE)
        total = own_ref[b, HD + 1 : HD + 2, :] * factor_a + other_ref[b, HD + 1 : HD + 2, :] * factor_b
        result = (own_ref[b, :HD, :] * factor_a + other_ref[b, :HD, :] * factor_b) / total
        for i in range(LANES // ROWS):
            h = b * (LANES // ROWS) + i
            out_ref[:, h * HD : (h + 1) * HD] = result[:, i * ROWS : (i + 1) * ROWS].T.astype(jnp.bfloat16)


STATE = jax.ShapeDtypeStruct((CORE, PARTS, STATE_ROWS, LANES), jnp.float32)
HALF_STATE = jax.ShapeDtypeStruct((PARTS, STATE_ROWS, LANES), jnp.float32)


def call_pack(place, *parts):
    return pl.pallas_call(
        pack,
        out_shape=jax.ShapeDtypeStruct((2 * BLOCK_KEYS, HD), jnp.bfloat16),
        in_specs=[SMEM] + [VMEM] * 3,
        out_specs=VMEM,
        compiler_params=PARAMS,
        name="pack",
    )(place, *parts)


def call_plan(place, prefix_lengths, span_seg, queries, sib_queries):
    return pl.pallas_call(
        plan,
        out_shape=(
            jax.ShapeDtypeStruct((CORE * 8,), jnp.int32),
            jax.ShapeDtypeStruct((CORE, 8, ROWS), jnp.int32),
            jax.ShapeDtypeStruct((CORE, PARTS, HD, LANES), jnp.bfloat16),
        ),
        in_specs=[SMEM, SMEM, VMEM, VMEM, VMEM],
        out_specs=(SMEM, VMEM, VMEM),
        compiler_params=PARAMS,
        name="plan",
    )(place, prefix_lengths, span_seg.reshape(-1, ROWS), queries, sib_queries)


def call_absorb(step, turned, place, planned, block, state):
    final = step == STEPS
    return pl.pallas_call(
        functools.partial(absorb_step, step, turned, final),
        out_shape=(STATE, HALF_STATE, HALF_STATE) if final else STATE,
        in_specs=[SMEM, SMEM, VMEM, VMEM, VMEM] + ([VMEM] if step else []),
        out_specs=(VMEM,) * 3 if final else VMEM,
        input_output_aliases={5: 0} if step else {},
        compiler_params=PARAMS,
        cost_estimate=pl.CostEstimate(flops=400_000_000, bytes_accessed=2_000_000, transcendentals=790_000),
        name="absorb",
    )(place, *planned, block, *([state] if step else []))


def call_merge(own, other):
    return pl.pallas_call(
        merge,
        out_shape=jax.ShapeDtypeStruct((ROWS, GROUP * HD), jnp.bfloat16),
        in_specs=[VMEM, VMEM],
        out_specs=VMEM,
        compiler_params=PARAMS,
        name="merge",
    )(own, other)


def at(xh, z, core):
    return (xh * Z + z) * CORE + core


def body(queries, span_keys, span_values, prefix_keys, prefix_values, span_seg, prefix_lengths):
    place = jnp.stack([lax.axis_index(a) for a in INST]).astype(jnp.int32)
    everyone = [(xh, z, c) for xh in range(XH) for z in range(Z) for c in range(CORE)]
    sibling = [(at(xh, z, c), at(xh, z, 1 - c)) for xh, z, c in everyone]
    across = [(at(xh, z, c), at(1 - xh, z, c)) for xh, z, c in everyone]
    ways = [[(at(xh, z, c), at(xh, (z + sign * (1 - 2 * c)) % Z, c)) for xh, z, c in everyone] for sign in (1, -1)]

    pre = jnp.concatenate(
        [prefix_keys.reshape(-1, KV_HEADS, HD), prefix_values.reshape(-1, KV_HEADS, HD)], axis=2
    ).transpose(1, 0, 2)
    pre = jnp.broadcast_to(pre[None], (XH,) + pre.shape).reshape((XH * TP,) + pre.shape[1:])
    pre = lax.all_to_all(pre, ("xh", "tp"), split_axis=0, concat_axis=0, tiled=True)
    pre = pre.reshape(XH * PIECE, 2 * HD)

    span = jnp.stack([span_keys, span_values])
    held = call_pack(place, span, lax.ppermute(span, INST, across), pre)
    planned = call_plan(place, prefix_lengths, span_seg, queries, lax.ppermute(queries, INST, sibling))

    blocks = [lax.ppermute(held, INST, way) for way in ways]
    state = call_absorb(0, False, place, planned, held, None)
    for step in range(1, STEPS):
        for i, way in enumerate(ways):
            block, state = lax.optimization_barrier((blocks[i], state))
            if step < STEPS - 1 or i == 0:
                blocks[i] = lax.ppermute(block, INST, way)
            state = call_absorb(step, i == 1, place, planned, block, state)
    _, own, sib = call_absorb(STEPS, False, place, planned, *lax.optimization_barrier((blocks[0], state)))
    return call_merge(own, lax.ppermute(sib, INST, sibling))


def solution(mesh):
    cut = Mesh(mesh.devices.reshape(XH, Z, CORE, TP), INST + ("tp",))
    in_specs = (
        P(INST, "tp"),
        P(INST, "tp"),
        P(INST, "tp"),
        P(INST + ("tp",), None),
        P(INST + ("tp",), None),
        P(),
        P(),
    )
    return jax.shard_map(body, mesh=cut, in_specs=in_specs, out_specs=P(INST, "tp"), check_vma=False)
```

```python
import functools
import math

import jax
import jax.numpy as jnp
from jax import lax
from jax.experimental import pallas as pl
from jax.experimental.pallas import tpu as pltpu
from jax.sharding import Mesh, PartitionSpec as P

HEADS = 64
KV_HEADS = 8
HD = 128
GROUP = HEADS // KV_HEADS
REQ = 4
SPAN = 8192
PREFIX = 4096
XH, Z, CORE, TP = 2, 16, 2, 8
CHIPS = XH * Z
INST = ("xh", "z", "core")
ROWS = SPAN // (CHIPS * CORE)
KEYS = ROWS * CORE
PIECE = PREFIX // CHIPS
BLOCK_KEYS = KEYS + PIECE
LANES = 2 * ROWS
PARTS = GROUP * ROWS // LANES
STEPS = Z // 2
STATE_ROWS = HD + 8
LOW = -1e30
EXP2_SCALE = math.log2(math.e) / math.sqrt(HD)

SMEM = pl.BlockSpec(memory_space=pltpu.SMEM)
VMEM = pl.BlockSpec(memory_space=pltpu.VMEM)
PARAMS = pltpu.CompilerParams(vmem_limit_bytes=24 * 1024 * 1024)


def turn(tile):
    return tile.astype(jnp.float32).T.astype(jnp.bfloat16)


def collect(place_ref, own_ref, across_ref, pre_ref, rows_ref):
    for xh in range(XH):
        for i in range(2):
            tile = jnp.where(place_ref[0] == xh, own_ref[i], across_ref[i])
            rows_ref[xh * ROWS : (xh + 1) * ROWS, i * HD : (i + 1) * HD] = tile
    rows_ref[XH * ROWS :, :] = pre_ref[...]


def pack(place_ref, own_ref, sib_ref, *block_refs):
    half = PIECE // CORE
    for xh in range(XH):
        shares = []
        for core in range(CORE):
            mine = place_ref[2] == core
            first = xh * ROWS
            rows = jnp.where(mine, own_ref[first : first + ROWS, :], sib_ref[first : first + ROWS, :])
            block_refs[xh][core * ROWS : (core + 1) * ROWS, :] = rows[:, :HD]
            block_refs[xh][BLOCK_KEYS + core * HD : BLOCK_KEYS + (core + 1) * HD, :] = turn(rows[:, HD:])
            first = XH * ROWS + xh * half
            shares.append(jnp.where(mine, own_ref[first : first + half, :], sib_ref[first : first + half, :]))
        rows = jnp.concatenate(shares, axis=0)
        block_refs[xh][KEYS:BLOCK_KEYS, :] = rows[:, :HD]
        block_refs[xh][BLOCK_KEYS + KEYS :, :] = turn(rows[:, HD:])


def plan(place_ref, lengths_ref, seg_ref, q_ref, sib_ref, scalars_ref, bounds_ref, rows_ref):
    inst = (place_ref[0] * Z + place_ref[1]) * CORE + place_ref[2]
    sibling = inst + 1 - 2 * place_ref[2]
    seg = seg_ref[...]
    counts = [jnp.int32(0)] + [
        jnp.sum(jnp.where(seg < s, 1.0, 0.0)).astype(jnp.int32) for s in range(1, REQ)
    ]
    starts, ends, running = [], [], jnp.int32(0)
    for s in range(REQ):
        starts.append(running)
        running = running + lengths_ref[s]
        ends.append(running)

    def pick(values, s):
        out = values[0]
        for k in range(1, REQ):
            out = jnp.where(s == k, values[k], out)
        return out

    for half, block in enumerate((inst, sibling)):
        first = block * ROWS
        first_seg, last_seg = jnp.int32(0), jnp.int32(0)
        for s in range(1, REQ):
            first_seg = first_seg + (first >= counts[s]).astype(jnp.int32)
            last_seg = last_seg + (first + ROWS - 1 >= counts[s]).astype(jnp.int32)
        values = (
            pick(starts, first_seg), pick(ends, last_seg), pick(starts, last_seg), pick(ends, first_seg),
            pick(counts, first_seg), first + ROWS, pick(counts, last_seg), first + 1,
        )
        for i, value in enumerate(values):
            scalars_ref[half * 8 + i] = value
        position = first + lax.broadcasted_iota(jnp.int32, (1, ROWS), 1)
        row_seg = jnp.zeros((1, ROWS), jnp.int32)
        for s in range(1, REQ):
            row_seg = row_seg + jnp.where(position >= counts[s], 1, 0)
        bounds_ref[half, 0:1, :] = pick(starts, row_seg)
        bounds_ref[half, 1:2, :] = pick(ends, row_seg)
        bounds_ref[half, 2:3, :] = pick(counts, row_seg)
        bounds_ref[half, 3:4, :] = position + 1
        ref = (q_ref, sib_ref)[half]
        for h in range(GROUP):
            rows_ref[half, h // 2, :, h % 2 * ROWS : (h % 2 + 1) * ROWS] = turn(ref[:, h * HD : (h + 1) * HD])


def absorb_step(step, which, final, place_ref, scalars_ref, bounds_ref, rows_ref, block_ref, *refs):
    core, z = place_ref[2], place_ref[1]
    origin = lax.rem(jnp.where(core == 0, z - step + Z, z + step), Z)
    xh = core if which is None else which
    if final:
        _, state, own_ref, sib_ref = refs
    else:
        state = refs[-1]
    if step == 0:
        state[:, :, :HD, :] = jnp.zeros((CORE, PARTS, HD, LANES), jnp.float32)
        state[:, :, HD:, :] = jnp.zeros((CORE, PARTS, STATE_ROWS - HD, LANES), jnp.float32)
        state[:, :, HD : HD + 1, :] = jnp.full((CORE, PARTS, 1, LANES), LOW, jnp.float32)

    def absorb(half, row, count, base, kind, masked):
        keys = block_ref[row : row + count, :]
        vals = jnp.concatenate(
            [block_ref[BLOCK_KEYS + i : BLOCK_KEYS + i + HD, :] for i in range(row, row + count, HD)], axis=1
        )
        every = range(PARTS)
        scores = [jnp.dot(keys, rows_ref[half, b], preferred_element_type=jnp.float32) for b in every]
        if masked:
            index = base + lax.broadcasted_iota(jnp.int32, (count, ROWS), 0)
            low = bounds_ref[half, 2 * kind : 2 * kind + 1, :]
            high = bounds_ref[half, 2 * kind + 1 : 2 * kind + 2, :]
            bias = jnp.where((index >= low) & (index < high), 0.0, LOW)
            bias = jnp.concatenate([bias] * (LANES // ROWS), axis=1)
            scores = [scores[b] + bias for b in every]
        old = [state[half, b, HD : HD + 1, :] for b in every]
        new = [jnp.maximum(old[b], jnp.max(scores[b], axis=0, keepdims=True)) for b in every]
        factor = [jnp.exp2((old[b] - new[b]) * EXP2_SCALE) for b in every]
        expo = [jnp.exp2((scores[b] - new[b]) * EXP2_SCALE) for b in every]
        total = [
            state[half, b, HD + 1 : HD + 2, :] * factor[b] + jnp.sum(expo[b], axis=0, keepdims=True) for b in every
        ]
        summed = [
            state[half, b, :HD, :] * factor[b]
            + jnp.dot(vals, expo[b].astype(jnp.bfloat16), preferred_element_type=jnp.float32)
            for b in every
        ]
        for b in every:
            state[half, b, :HD, :] = summed[b]
            state[half, b, HD : HD + 1, :] = new[b]
            state[half, b, HD + 1 : HD + 2, :] = total[b]

    def visit(half, row, count, base, kind):
        least_lo, most_hi, most_lo, least_hi = [scalars_ref[half * 8 + kind * 4 + i] for i in range(4)]
        seen = (base < most_hi) & (base + count > least_lo)
        if step == STEPS:
            seen = seen & (core == 1)
        whole = (base >= most_lo) & (base + count <= least_hi)

        @pl.when(seen & whole)
        def _():
            absorb(half, row, count, base, kind, False)

        @pl.when(seen & jnp.logical_not(whole))
        def _():
            absorb(half, row, count, base, kind, True)

    def one_half(half, carry):
        visit(half, 0, KEYS, (xh * Z + origin) * KEYS, 1)
        visit(half, KEYS, PIECE, (xh * Z + origin) * PIECE, 0)
        return carry

    lax.fori_loop(0, CORE, one_half, 0)
    if final:
        own_ref[...] = state[0]
        sib_ref[...] = state[1]


def merge(own_ref, other_ref, out_ref):
    for b in range(PARTS):
        top_a, top_b = own_ref[b, HD : HD + 1, :], other_ref[b, HD : HD + 1, :]
        top = jnp.maximum(top_a, top_b)
        factor_a = jnp.exp2((top_a - top) * EXP2_SCALE)
        factor_b = jnp.exp2((top_b - top) * EXP2_SCALE)
        total = own_ref[b, HD + 1 : HD + 2, :] * factor_a + other_ref[b, HD + 1 : HD + 2, :] * factor_b
        result = (own_ref[b, :HD, :] * factor_a + other_ref[b, :HD, :] * factor_b) / total
        for i in range(LANES // ROWS):
            h = b * (LANES // ROWS) + i
            out_ref[:, h * HD : (h + 1) * HD] = result[:, i * ROWS : (i + 1) * ROWS].T.astype(jnp.bfloat16)


STATE = jax.ShapeDtypeStruct((CORE, PARTS, STATE_ROWS, LANES), jnp.float32)
HALF_STATE = jax.ShapeDtypeStruct((PARTS, STATE_ROWS, LANES), jnp.float32)


def call_collect(place, own, across, pre):
    return pl.pallas_call(
        collect,
        out_shape=jax.ShapeDtypeStruct((BLOCK_KEYS, 2 * HD), jnp.bfloat16),
        in_specs=[SMEM] + [VMEM] * 3,
        out_specs=VMEM,
        compiler_params=PARAMS,
        name="collect",
    )(place, own, across, pre)


def call_pack(place, own, sib):
    return pl.pallas_call(
        pack,
        out_shape=(jax.ShapeDtypeStruct((2 * BLOCK_KEYS, HD), jnp.bfloat16),) * XH,
        in_specs=[SMEM] + [VMEM] * 2,
        out_specs=(VMEM,) * XH,
        compiler_params=PARAMS,
        name="pack",
    )(place, own, sib)


def call_plan(place, prefix_lengths, span_seg, queries, sib_queries):
    return pl.pallas_call(
        plan,
        out_shape=(
            jax.ShapeDtypeStruct((CORE * 8,), jnp.int32),
            jax.ShapeDtypeStruct((CORE, 8, ROWS), jnp.int32),
            jax.ShapeDtypeStruct((CORE, PARTS, HD, LANES), jnp.bfloat16),
        ),
        in_specs=[SMEM, SMEM, VMEM, VMEM, VMEM],
        out_specs=(SMEM, VMEM, VMEM),
        compiler_params=PARAMS,
        name="plan",
    )(place, prefix_lengths, span_seg.reshape(-1, ROWS), queries, sib_queries)


def call_absorb(step, which, place, planned, block, state):
    final = step == STEPS and which == XH - 1
    return pl.pallas_call(
        functools.partial(absorb_step, step, which, final),
        out_shape=(STATE, HALF_STATE, HALF_STATE) if final else STATE,
        in_specs=[SMEM, SMEM, VMEM, VMEM, VMEM] + ([VMEM] if step else []),
        out_specs=(VMEM,) * 3 if final else VMEM,
        input_output_aliases={5: 0} if step else {},
        compiler_params=PARAMS,
        cost_estimate=pl.CostEstimate(flops=400_000_000, bytes_accessed=2_000_000, transcendentals=790_000),
        name="absorb",
    )(place, *planned, block, *([state] if step else []))


def call_merge(own, other):
    return pl.pallas_call(
        merge,
        out_shape=jax.ShapeDtypeStruct((ROWS, GROUP * HD), jnp.bfloat16),
        in_specs=[VMEM, VMEM],
        out_specs=VMEM,
        compiler_params=PARAMS,
        name="merge",
    )(own, other)


def at(xh, z, core):
    return (xh * Z + z) * CORE + core


def body(queries, span_keys, span_values, prefix_keys, prefix_values, span_seg, prefix_lengths):
    place = jnp.stack([lax.axis_index(a) for a in INST]).astype(jnp.int32)
    everyone = [(xh, z, c) for xh in range(XH) for z in range(Z) for c in range(CORE)]
    sibling = [(at(xh, z, c), at(xh, z, 1 - c)) for xh, z, c in everyone]
    across = [(at(xh, z, c), at(1 - xh, z, c)) for xh, z, c in everyone]
    along = [(at(xh, z, c), at(xh, (z + 1 - 2 * c) % Z, c)) for xh, z, c in everyone]
    down = [way for way in along if way[0] % CORE == 1]

    pre = jnp.concatenate(
        [prefix_keys.reshape(-1, KV_HEADS, HD), prefix_values.reshape(-1, KV_HEADS, HD)], axis=2
    ).transpose(1, 0, 2)
    pre = jnp.broadcast_to(pre[None], (XH,) + pre.shape).reshape((XH * TP,) + pre.shape[1:])
    pre = lax.all_to_all(pre, ("xh", "tp"), split_axis=0, concat_axis=0, tiled=True)
    pre = pre.reshape(PIECE, 2 * HD)

    span = jnp.stack([span_keys, span_values])
    rows = call_collect(place, span, lax.ppermute(span, INST, across), pre)
    blocks = list(call_pack(place, rows, lax.ppermute(rows, INST, sibling)))
    planned = call_plan(place, prefix_lengths, span_seg, queries, lax.ppermute(queries, INST, sibling))

    mine = jnp.where(place[2] == 0, blocks[0], blocks[1])
    blocks = [lax.ppermute(block, INST, along) for block in blocks]
    state = call_absorb(0, None, place, planned, mine, None)
    for step in range(1, STEPS + 1):
        for xh in range(XH):
            block, state = lax.optimization_barrier((blocks[xh], state))
            if step < STEPS:
                blocks[xh] = lax.ppermute(block, INST, along if step < STEPS - 1 else down)
            state = call_absorb(step, xh, place, planned, block, state)
    _, own, sib = state
    return call_merge(own, lax.ppermute(sib, INST, sibling))


def solution(mesh):
    cut = Mesh(mesh.devices.reshape(XH, Z, CORE, TP), INST + ("tp",))
    in_specs = (
        P(INST, "tp"),
        P(INST, "tp"),
        P(INST, "tp"),
        P(INST + ("tp",), None),
        P(INST + ("tp",), None),
        P(),
        P(),
    )
    return jax.shard_map(body, mesh=cut, in_specs=in_specs, out_specs=P(INST, "tp"), check_vma=False)
```
